128 devices in a mesh: pipe: 4 (over y_hi, core), dp: 32 (over x, y_lo, z).
Axes of the slice: x: 4, y: 4 (y_hi: 2, y_lo: 2; y = y_hi * 2 + y_lo), z: 4, core: 2. Of those that a mesh axis runs over, the one named last changes fastest.
Arguments:
- enc_out: bfloat16 [4, 4096, 2048], P('pipe', 'dp'), may hold values from -6 to 6
- kv_weight: bfloat16 [4, 2048, 4096], P('pipe'), may hold values from -0.125 to 0.125
- queries: bfloat16 [4, 4, 1024, 2048], P('pipe', None, 'dp'), may hold values from -0.375 to 0.375
- out_grad: bfloat16 [4, 4, 1024, 2048], P('pipe', None, 'dp'), may hold values from -24 to 24
Outputs:
- grad_kv: float32 [4, 2048, 4096], P('pipe', 'dp')
- grad_enc: float32 [4, 4096, 2048], P('pipe', 'dp')
- grad_query: bfloat16 [4, 4, 1024, 2048], P('pipe', None, 'dp')
The draws below stay inside these ranges and needn't reach their ends.
All inputs are finite; a program needn't handle non-finite values.
Results may differ from the reference program's by a relative error of at most 0.013.
Values may be sent and summed in bfloat16 or wider, within the bound.
A program may use at most 192 MiB of HBM per device.

```python
import jax
import jax.numpy as jnp
from jax import lax

D = 2048
HEADS = 8
HD = 256
INNER = 2048
ENC_LEN = 128
DEC_LEN = 32
MICRO = 4
ENC_ROWS = 4096
DEC_ROWS = 1024
N_PIPE = 4
N_DP = 32


def with_spikes(array, key, source, target, blocks, factor):
    owner, partner = [(jnp.arange(array.shape[dim]) // (array.shape[dim] // blocks)).reshape([-1 if axis == dim else 1 for axis in range(array.ndim)]) for dim in (source, target)]
    chosen = jax.random.permutation(key, blocks)[partner]
    strong = (owner == chosen) | (owner == (partner + blocks // 2) % blocks)
    return jnp.where(strong, factor * array, array)


def levels(own_key, dims, pieces, low, largest):
    def one(axis_at, shards_of):
        heights = jax.random.uniform(jax.random.fold_in(jax.random.fold_in(own_key, 6), axis_at), (shards_of,), jnp.float32, low / len(pieces), largest / len(pieces))
        return jnp.repeat(jnp.exp(heights), dims[axis_at] // shards_of).reshape((-1,) + (1,) * (len(dims) - axis_at - 1))

    level = one(*pieces[0])
    for cut in pieces[1:]:
        level = level * one(*cut)
    return level


def gaussian(stream_key, dims, deviation, reach, cuts=(), dtype=jnp.bfloat16):
    drawn = deviation * jax.random.normal(stream_key, dims, jnp.float32)
    if cuts:
        drawn = drawn * levels(stream_key, dims, cuts, -0.22, 0.18)
    return jnp.clip(drawn, -reach, reach).astype(dtype)


def heavy_noise(stream_key, shape, deviation, most, split, heavy, kind=jnp.bfloat16):
    values = deviation * jax.random.normal(stream_key, shape, jnp.float32)
    if split:
        values = values * levels(stream_key, shape, split, -0.22, 0.18)
    return jnp.clip(with_spikes(values, jax.random.fold_in(stream_key, 3), *heavy), -most, most).astype(kind)


def setup_inputs(seed: int = 0) -> dict:
    arg_keys = jax.random.split(jax.random.key(seed), 5)
    enc_out = heavy_noise(arg_keys[0], (MICRO, ENC_ROWS, D), 1.0, 6.0, ((0, 4), (1, 32)), (1, 2, 32, 2.75))
    kv_weight = gaussian(arg_keys[1], (N_PIPE, D, 2 * INNER), D ** -0.5, 0.125, ((0, 4),))
    queries = gaussian(arg_keys[2], (N_PIPE, MICRO, DEC_ROWS, INNER), 0.0625, 0.375, ((0, 4), (2, 32)))
    out_grad = gaussian(arg_keys[3], (N_PIPE, MICRO, DEC_ROWS, INNER), 4.0, 24.0, ((0, 4), (2, 32)))
    return dict(enc_out=enc_out, kv_weight=kv_weight, queries=queries, out_grad=out_grad)


def attend_back(query_heads, key_value, grad_heads):
    lead = key_value.shape[:-2]
    length = key_value.shape[-2]
    key_heads = key_value[..., :INNER].reshape(lead + (length, HEADS, HD)).astype(jnp.float32)
    value_heads = key_value[..., INNER:].reshape(lead + (length, HEADS, HD)).astype(jnp.float32)
    highest = lax.Precision.HIGHEST
    raw_scores = jnp.einsum("...qhd,...khd->...hqk", query_heads, key_heads, precision=highest)
    attn_probs = jax.nn.softmax(raw_scores, axis=-1)
    probs_low = attn_probs.astype(jnp.bfloat16).astype(jnp.float32)
    prob_grad = jnp.einsum("...qhd,...khd->...hqk", grad_heads, value_heads, precision=highest)
    row_total = jnp.sum(attn_probs * prob_grad, axis=-1, keepdims=True)
    score_grad = attn_probs * (prob_grad - row_total)
    score_low = score_grad.astype(jnp.bfloat16).astype(jnp.float32)
    query_grad = jnp.einsum("...hqk,...khd->...qhd", score_low, key_heads, precision=highest).astype(jnp.bfloat16)
    key_grad = jnp.einsum("...hqk,...qhd->...khd", score_low, query_heads, precision=highest).astype(jnp.bfloat16)
    value_grad = jnp.einsum("...hqk,...qhd->...khd", probs_low, grad_heads, precision=highest).astype(jnp.bfloat16)
    kv_grad = jnp.concatenate([key_grad.reshape(lead + (length, INNER)), value_grad.reshape(lead + (length, INNER))], axis=-1)
    return query_grad, kv_grad


def reference(enc_out, kv_weight, queries, out_grad):
    micro = enc_out.shape[0]
    enc_rows = enc_out.reshape(-1, D)
    grad_enc = jnp.zeros((micro * N_DP * ENC_LEN, D), jnp.float32)
    weight_grads = []
    query_grads = []
    for section in range(N_PIPE):
        weight = kv_weight[section]
        key_value = jnp.dot(enc_rows, weight, preferred_element_type=jnp.float32).astype(jnp.bfloat16)
        key_value = key_value.reshape(micro, N_DP, ENC_LEN, 2 * INNER)
        query_heads = queries[section].reshape(micro, N_DP, DEC_LEN, HEADS, HD).astype(jnp.float32)
        grad_heads = out_grad[section].reshape(micro, N_DP, DEC_LEN, HEADS, HD).astype(jnp.float32)
        query_grad, kv_grad = attend_back(query_heads, key_value, grad_heads)
        query_grads.append(query_grad.reshape(micro, N_DP * DEC_LEN, INNER))
        kv_rows = kv_grad.reshape(-1, 2 * INNER)
        weight_grads.append(jnp.dot(enc_rows.T, kv_rows, preferred_element_type=jnp.float32))
        grad_enc = grad_enc + jnp.dot(kv_rows, weight.T, preferred_element_type=jnp.float32)
    return (jnp.stack(weight_grads), grad_enc.reshape(micro, N_DP * ENC_LEN, D), jnp.stack(query_grads))
```

```python
import jax
import jax.numpy as jnp
from jax import lax
from jax.experimental import pallas as pl
from jax.experimental.pallas import tpu as pltpu
from jax.sharding import PartitionSpec as P

HD = 256
INNER = 2048
D = 2048
LEN = 128
Q = 32
BF = jnp.bfloat16
F32 = jnp.float32
MESH = pl.DeviceIdType.MESH

ENC, QG, SC, P1, P2, P3, E1, E2, NSEM = 0, 7, 15, 19, 43, 67, 75, 79, 83


def body(enc_hbm, w_hbm, q_hbm, g_hbm, gkv_hbm, genc_hbm, gq_hbm,
         w, encb, enct, kv, qb, gb, qgn, gqb, sco, sci, rhs, part, r1, r2, x3, r3, outb,
         ek, es, er, ys, yr, lsem, wsem, ssem, rsem):
    p = lax.axis_index("pipe")
    d = lax.axis_index("dp")
    yh, c = p // 2, p % 2
    x, yl, z = d // 8, (d // 4) % 2, d % 4
    po = 2 * yh + 1 - c
    pp = 2 * (1 - yh) + c
    ppo = 2 * (1 - yh) + 1 - c
    dn = x * 8 + (1 - yl) * 4 + z
    core, partner, near, far = (po, d), (pp, d), (p, dn), (pp, dn)

    def peer(half_axis, k):
        if half_axis == 0:
            return (p, lax.rem(x + k, 4) * 8 + yl * 4 + z)
        return (p, x * 8 + yl * 4 + lax.rem(z + k, 4))

    def rc(src, dst, idx, dev):
        return pltpu.make_async_remote_copy(
            src_ref=src, dst_ref=dst, send_sem=ssem.at[idx], recv_sem=rsem.at[idx],
            device_id=dev, device_id_type=MESH)

    def got(dst, idx):
        rc(dst, dst, idx, core).wait_recv()

    def w_copy(j):
        cols = pl.ds(pl.multiple_of(j * 256, 256), 256)
        return pltpu.make_async_copy(w_hbm.at[0, :, cols], w.at[:, cols], wsem.at[j])

    own_enc = pltpu.make_async_copy(enc_hbm.at[0], encb.at[p], lsem.at[0])
    own_q = pltpu.make_async_copy(q_hbm.at[0], qb, lsem.at[1])
    own_g = pltpu.make_async_copy(g_hbm.at[0], gb, lsem.at[2])
    own_enc.start()

    @pl.loop(0, 16)
    def _(j):
        w_copy(j).start()

    own_q.start()
    own_g.start()

    barrier = pltpu.get_barrier_semaphore()
    others = [core, partner, near, far] + [peer(h, k) for h in (0, 1) for k in (1, 2, 3)]
    for dev in others:
        pl.semaphore_signal(barrier, inc=1, device_id=dev, device_id_type=MESH)
    pl.semaphore_wait(barrier, len(others))

    sends = []

    def send(src, dst, idx, dev):
        cp = rc(src, dst, idx, dev)
        cp.start()
        sends.append(cp)

    send(enc_hbm.at[0], encb.at[p], ENC + 0, core)
    send(enc_hbm.at[0], encb.at[p], ENC + 1, partner)

    def project(first, j):
        cols = pl.ds(pl.multiple_of(j * 256, 256), 256)
        rows = encb[pl.ds(first, 2)].reshape(256, D)
        out = jnp.dot(rows, w[:, cols], preferred_element_type=F32)
        kv[pl.ds(first, 2), :, cols] = out.astype(BF).reshape(2, LEN, 256)

    def transpose(slot):
        cols = pl.ds(pl.multiple_of(slot * LEN, LEN), LEN)

        @pl.loop(0, 8)
        def _(b):
            rows = pl.ds(pl.multiple_of(b * 256, 256), 256)
            enct[rows, cols] = encb[slot, :, rows].T

    own_enc.wait()
    got(encb.at[po], ENC + 0)

    @pl.loop(0, 16)
    def _(j):
        w_copy(j).wait()
        project(2 * yh, j)

    own_q.wait()
    own_g.wait()
    send(enc_hbm.at[0], encb.at[4 + p], ENC + 2, near)
    send(enc_hbm.at[0], encb.at[4 + p], ENC + 3, far)
    for i in range(4):
        cols = pl.ds(pl.multiple_of((1 - yl) * 1024 + i * 256, 256), 256)
        send(qb.at[:, :, cols], qgn.at[i, 0], QG + 2 * i, near)
        send(gb.at[:, :, cols], qgn.at[i, 1], QG + 2 * i + 1, near)
    transpose(p)
    transpose(po)
    got(encb.at[pp], ENC + 1)
    send(encb.at[pp], encb.at[pp], ENC + 4, core)
    transpose(pp)
    got(encb.at[ppo], ENC + 4)
    transpose(ppo)

    tl = (((0,), (0,)), ((), ()))
    nt = (((1,), (1,)), ((), ()))

    def attend(i, slot):
        @pl.loop(0, 4)
        def _(t):
            project(2 * (1 - yh), i + 4 * t)

        units = []
        for own in (0, 1):
            head = (yl if own else 1 - yl) * 4 + i
            kc = pl.ds(pl.multiple_of(head * HD, HD), HD)
            vc = pl.ds(pl.multiple_of(INNER + head * HD, HD), HD)
            for m in range(4):
                units.append((own, kc, vc, m))
        raws, pgs = [], []
        for own, kc, vc, m in units:
            raws.append(lax.dot_general(qb[m, :, kc], kv[m, :, kc], nt, preferred_element_type=F32))
            pgs.append(lax.dot_general(gb[m, :, kc], kv[m, :, vc], nt, preferred_element_type=F32))
        raw = jnp.concatenate(raws, axis=0)
        pg = jnp.concatenate(pgs, axis=0)
        e = jnp.exp(raw - jnp.max(raw, axis=-1, keepdims=True))
        prob = e / jnp.sum(e, axis=-1, keepdims=True)
        total = jnp.sum(prob * pg, axis=-1, keepdims=True)
        score = (prob * (pg - total)).astype(BF)
        low = prob.astype(BF)
        for n, (own, kc, vc, m) in enumerate(units):
            s_n, p_n = score[n * Q:(n + 1) * Q], low[n * Q:(n + 1) * Q]
            gqb[m, :, kc] = jnp.dot(s_n, kv[m, :, kc], preferred_element_type=F32).astype(BF)
            kg = lax.dot_general(s_n, qb[m, :, kc], tl, preferred_element_type=F32).astype(BF)
            vg = lax.dot_general(p_n, gb[m, :, kc], tl, preferred_element_type=F32).astype(BF)
            kv[m, :, kc] = kg
            kv[m, :, vc] = vg
            if own:
                rhs[slot, m * LEN:(m + 1) * LEN, 0:HD] = kg
                rhs[slot, m * LEN:(m + 1) * LEN, HD:2 * HD] = vg
            else:
                sco[i, 0, m] = s_n
                sco[i, 1, m] = p_n
        send(sco.at[i], sci.at[i], SC + i, near)

    def weight(i, slot):
        got(sci.at[i], SC + i)
        got(qgn.at[i, 0], QG + 2 * i)
        got(qgn.at[i, 1], QG + 2 * i + 1)
        for m in range(4):
            kg = lax.dot_general(sci[i, 0, m], qgn[i, 0, m], tl, preferred_element_type=F32)
            vg = lax.dot_general(sci[i, 1, m], qgn[i, 1, m], tl, preferred_element_type=F32)
            rhs[slot, 512 + m * LEN:512 + (m + 1) * LEN, 0:HD] = kg.astype(BF)
            rhs[slot, 512 + m * LEN:512 + (m + 1) * LEN, HD:2 * HD] = vg.astype(BF)

        @pl.loop(0, 4)
        def _(xp):
            rows = pl.ds(pl.multiple_of(xp * 512, 512), 512)
            for half in (0, 1):
                out = jnp.dot(enct[rows, :], rhs[slot, :, half * HD:(half + 1) * HD],
                              preferred_element_type=F32).astype(BF)
                for yy in range(2):
                    for zz in range(4):
                        piece = out[yy * 256 + zz * 64:yy * 256 + zz * 64 + 64]
                        if half == 0:
                            part[i, 0, xp, zz * 128 + yy * 64:zz * 128 + yy * 64 + 64] = piece
                        else:
                            at = pl.multiple_of(xp * 128 + yy * 64, 64)
                            part[i, 1, zz, pl.ds(at, 64)] = piece

    first = (x, z)
    second = (z, x)

    def send1(i):
        for half in (0, 1):
            for k in (1, 2, 3):
                send(part.at[i, half, lax.rem(first[half] + k, 4)], r1.at[i, half, k - 1],
                     P1 + (2 * i + half) * 3 + k - 1, peer(half, k))

    def reduce1(i):
        for half in (0, 1):
            a = first[half]
            for k in (1, 2, 3):
                got(r1.at[i, half, k - 1], P1 + (2 * i + half) * 3 + k - 1)

            @pl.loop(0, 8)
            def _(b):
                rows = pl.ds(pl.multiple_of(b * 64, 64), 64)
                acc = part[i, half, a, rows].astype(F32)
                for k in range(3):
                    acc += r1[i, half, k, rows].astype(F32)
                part[i, half, a, rows] = acc.astype(BF)

            for k in (1, 2, 3):
                rows = pl.ds(pl.multiple_of(lax.rem(second[half] + k, 4) * 128, 128), 128)
                send(part.at[i, half, a, rows], r2.at[i, half, k - 1],
                     P2 + (2 * i + half) * 3 + k - 1, peer(1 - half, k))

    def reduce2(i):
        for half in (0, 1):
            a = first[half]
            for k in (1, 2, 3):
                got(r2.at[i, half, k - 1], P2 + (2 * i + half) * 3 + k - 1)

            def total(which):
                at = pl.ds(pl.multiple_of(second[half] * 128 + which * 64, 64), 64)
                rows = pl.ds(pl.multiple_of(which * 64, 64), 64)
                acc = part[i, half, a, at].astype(F32)
                for k in range(3):
                    acc += r2[i, half, k, rows].astype(F32)
                return acc

            x3[i, half] = total(1 - yl).astype(BF)
            send(x3.at[i, half], r3.at[i, half], P3 + 2 * i + half, near)
            cols = pl.ds(pl.multiple_of(half * INNER + (yl * 4 + i) * HD, HD), HD)
            outb[:, cols] = total(yl)

    def finish(i):
        for half in (0, 1):
            got(r3.at[i, half], P3 + 2 * i + half)
            cols = pl.ds(pl.multiple_of(half * INNER + ((1 - yl) * 4 + i) * HD, HD), HD)
            outb[:, cols] = r3[i, half].astype(F32)

    def enc_term(piece):
        @pl.loop(0, 2)
        def _(t):
            cols = pl.ds(pl.multiple_of(piece * 512 + t * 256, 256), 256)
            out = lax.dot_general(kv[...].reshape(512, 2 * INNER), w[cols, :], nt,
                                  preferred_element_type=F32).reshape(4, LEN, 256)
            for u in (0, 1):
                ek[u, :, cols] = jnp.where(c == 0, out[2 * u], out[2 * u + 1])
                es[u, :, cols] = jnp.where(c == 0, out[2 * u + 1], out[2 * u]).astype(BF)

        cols = pl.ds(piece * 512, 512)
        send(es.at[:, :, cols], er.at[:, :, cols], E1 + piece, core)

    def enc_pair(piece):
        cols = pl.ds(piece * 512, 512)
        got(er.at[:, :, cols], E1 + piece)
        ys[:, cols] = (ek[1 - yh, :, cols] + er[1 - yh, :, cols].astype(F32)).astype(BF)
        send(ys.at[:, cols], yr.at[:, cols], E2 + piece, partner)
        ek[yh, :, cols] = ek[yh, :, cols] + er[yh, :, cols].astype(F32)

    def enc_last(piece):
        cols = pl.ds(piece * 512, 512)
        got(yr.at[:, cols], E2 + piece)
        ek[yh, :, cols] = ek[yh, :, cols] + yr[:, cols].astype(F32)

    attend(0, 0)
    attend(1, 1)
    got(encb.at[4 + p], ENC + 2)
    send(encb.at[4 + p], encb.at[4 + p], ENC + 5, core)
    transpose(4 + p)
    got(encb.at[4 + pp], ENC + 3)
    send(encb.at[4 + pp], encb.at[4 + pp], ENC + 6, core)
    transpose(4 + pp)
    got(encb.at[4 + po], ENC + 5)
    transpose(4 + po)
    got(encb.at[4 + ppo], ENC + 6)
    transpose(4 + ppo)
    weight(0, 0)
    send1(0)
    attend(2, 0)
    weight(1, 1)
    send1(1)
    attend(3, 1)
    out_q = pltpu.make_async_copy(gqb, gq_hbm.at[0], lsem.at[3])
    out_q.start()
    weight(2, 0)
    send1(2)
    weight(3, 1)
    send1(3)
    enc_term(0)
    enc_term(1)
    reduce1(0)
    enc_term(2)
    enc_pair(0)
    enc_term(3)
    enc_pair(1)
    reduce1(1)
    enc_pair(2)
    enc_pair(3)
    reduce2(0)
    reduce1(2)
    reduce2(1)
    for piece in range(4):
        enc_last(piece)
    out_e = pltpu.make_async_copy(ek.at[yh], genc_hbm.at[0], lsem.at[4])
    out_e.start()
    finish(0)
    reduce1(3)
    reduce2(2)
    finish(1)
    reduce2(3)
    finish(2)
    finish(3)
    out_w = pltpu.make_async_copy(outb, gkv_hbm.at[0], lsem.at[5])
    out_w.start()
    for cp in sends:
        cp.wait_send()
    out_q.wait()
    out_e.wait()
    out_w.wait()


def per_device(enc_out, kv_weight, queries, out_grad):
    anywhere = pl.BlockSpec(memory_space=pl.ANY)
    vm = pltpu.VMEM
    return pl.pallas_call(
        body,
        out_shape=(
            jax.ShapeDtypeStruct((1, 64, 2 * INNER), F32),
            jax.ShapeDtypeStruct((1, LEN, D), F32),
            jax.ShapeDtypeStruct((1, 4, Q, INNER), BF),
        ),
        in_specs=[anywhere] * 4,
        out_specs=(anywhere,) * 3,
        scratch_shapes=[
            vm((D, 2 * INNER), BF),
            vm((8, LEN, D), BF),
            vm((D, 8 * LEN), BF),
            vm((4, LEN, 2 * INNER), BF),
            vm((4, Q, INNER), BF),
            vm((4, Q, INNER), BF),
            vm((4, 2, 4, Q, HD), BF),
            vm((4, Q, INNER), BF),
            vm((4, 2, 4, Q, LEN), BF),
            vm((4, 2, 4, Q, LEN), BF),
            vm((2, 8 * LEN, 2 * HD), BF),
            vm((4, 2, 4, 512, HD), BF),
            vm((4, 2, 3, 512, HD), BF),
            vm((4, 2, 3, 128, HD), BF),
            vm((4, 2, 64, HD), BF),
            vm((4, 2, 64, HD), BF),
            vm((64, 2 * INNER), F32),
            vm((2, LEN, D), F32),
            vm((2, LEN, D), BF),
            vm((2, LEN, D), BF),
            vm((LEN, D), BF),
            vm((LEN, D), BF),
            pltpu.SemaphoreType.DMA((6,)),
            pltpu.SemaphoreType.DMA((16,)),
            pltpu.SemaphoreType.DMA((NSEM,)),
            pltpu.SemaphoreType.DMA((NSEM,)),
        ],
        compiler_params=pltpu.CompilerParams(
            collective_id=0, has_side_effects=True, vmem_limit_bytes=62 * 1024 * 1024),
        name="kv_backward",
    )(enc_out, kv_weight, queries, out_grad)


def solution(mesh):
    placed = (
        P("pipe", "dp", None),
        P("pipe", None, None),
        P("pipe", None, "dp", None),
        P("pipe", None, "dp", None),
    )
    return jax.shard_map(
        per_device,
        mesh=mesh,
        in_specs=placed,
        out_specs=(P("pipe", "dp", None), P("pipe", "dp", None), P("pipe", None, "dp", None)),
        check_vma=False,
    )
```

```python
import jax
import jax.numpy as jnp
from jax import lax
from jax.experimental import pallas as pl
from jax.experimental.pallas import tpu as pltpu
from jax.sharding import PartitionSpec as P

HD = 256
INNER = 2048
D = 2048
LEN = 128
Q = 32
BF = jnp.bfloat16
F32 = jnp.float32
MESH = pl.DeviceIdType.MESH

ENC, QG, SC, P1, P2, P3, E1, E2, NSEM = 0, 10, 18, 22, 70, 94, 102, 106, 110


def body(enc_hbm, w_hbm, q_hbm, g_hbm, gkv_hbm, genc_hbm, gq_hbm,
         w, encb, enct, kv, qb, gb, qgn, gqb, sco, sci, rhs, part, f1, r1, r2, x3, outb,
         ek, es, er, ys, yr, lsem, wsem, ssem, rsem):
    p = lax.axis_index("pipe")
    d = lax.axis_index("dp")
    yh, c = p // 2, p % 2
    x, yl, z = d // 8, (d // 4) % 2, d % 4
    po = 2 * yh + 1 - c
    pp = 2 * (1 - yh) + c
    ppo = 2 * (1 - yh) + 1 - c
    dn = x * 8 + (1 - yl) * 4 + z
    core, partner, near, far = (po, d), (pp, d), (p, dn), (pp, dn)

    def peer(half_axis, k):
        if half_axis == 0:
            return (p, lax.rem(x + k, 4) * 8 + yl * 4 + z)
        return (p, x * 8 + yl * 4 + lax.rem(z + k, 4))

    def rc(src, dst, idx, dev):
        return pltpu.make_async_remote_copy(
            src_ref=src, dst_ref=dst, send_sem=ssem.at[idx], recv_sem=rsem.at[idx],
            device_id=dev, device_id_type=MESH)

    def got(dst, idx):
        rc(dst, dst, idx, core).wait_recv()

    def w_copy(j):
        cols = pl.ds(pl.multiple_of(j * 256, 256), 256)
        return pltpu.make_async_copy(w_hbm.at[0, :, cols], w.at[:, cols], wsem.at[j])

    own_enc = pltpu.make_async_copy(enc_hbm.at[0], encb.at[p], lsem.at[0])
    own_q = pltpu.make_async_copy(q_hbm.at[0], qb, lsem.at[1])
    own_g = pltpu.make_async_copy(g_hbm.at[0], gb, lsem.at[2])
    own_enc.start()

    @pl.loop(0, 16)
    def _(j):
        w_copy(j).start()

    own_q.start()
    own_g.start()

    barrier = pltpu.get_barrier_semaphore()
    others = [core, partner, near, far] + [peer(h, k) for h in (0, 1) for k in (1, 2, 3)]
    for dev in others:
        pl.semaphore_signal(barrier, inc=1, device_id=dev, device_id_type=MESH)
    pl.semaphore_wait(barrier, len(others))

    sends = []

    def send(src, dst, idx, dev):
        cp = rc(src, dst, idx, dev)
        cp.start()
        sends.append(cp)

    top, low_rows = pl.ds(0, 64), pl.ds(64, 64)
    send(enc_hbm.at[0], encb.at[p], ENC + 0, core)
    send(enc_hbm.at[0, top], encb.at[4 + p, top], ENC + 1, near)
    send(enc_hbm.at[0, low_rows], encb.at[4 + p, low_rows], ENC + 3, far)
    send(enc_hbm.at[0, low_rows], encb.at[4 + p, low_rows], ENC + 2, near)
    send(enc_hbm.at[0, top], encb.at[4 + p, top], ENC + 4, far)

    def project(first, j):
        cols = pl.ds(pl.multiple_of(j * 256, 256), 256)
        rows = encb[pl.ds(first, 2)].reshape(256, D)
        out = jnp.dot(rows, w[:, cols], preferred_element_type=F32)
        kv[pl.ds(first, 2), :, cols] = out.astype(BF).reshape(2, LEN, 256)

    def transpose(slot):
        cols = pl.ds(pl.multiple_of(slot * LEN, LEN), LEN)

        @pl.loop(0, 8)
        def _(b):
            rows = pl.ds(pl.multiple_of(b * 256, 256), 256)
            enct[rows, cols] = encb[slot, :, rows].T

    own_enc.wait()
    got(encb.at[po], ENC + 0)

    def local_kv(lo, hi):
        @pl.loop(lo, hi)
        def _(j):
            w_copy(j).wait()
            project(2 * yh, j)

    local_kv(0, 8)
    transpose(p)
    transpose(po)
    got(encb.at[4 + p, top], ENC + 1)
    send(encb.at[4 + p, top], encb.at[p, top], ENC + 5, far)
    got(encb.at[4 + pp, low_rows], ENC + 3)
    send(encb.at[4 + pp, low_rows], encb.at[pp, low_rows], ENC + 6, near)
    own_q.wait()
    own_g.wait()
    for i in range(4):
        cols = pl.ds(pl.multiple_of((1 - yl) * 1024 + i * 256, 256), 256)
        send(qb.at[:, :, cols], qgn.at[i, 0], QG + 2 * i, near)
        send(gb.at[:, :, cols], qgn.at[i, 1], QG + 2 * i + 1, near)
    local_kv(8, 16)
    got(encb.at[4 + p, low_rows], ENC + 2)
    send(encb.at[4 + p], encb.at[4 + p], ENC + 7, core)
    got(encb.at[4 + pp, top], ENC + 4)
    send(encb.at[4 + pp], encb.at[4 + pp], ENC + 8, core)
    transpose(4 + p)
    transpose(4 + pp)
    got(encb.at[pp, top], ENC + 5)
    got(encb.at[pp, low_rows], ENC + 6)
    send(encb.at[pp], encb.at[pp], ENC + 9, core)
    transpose(pp)
    got(encb.at[4 + po], ENC + 7)
    transpose(4 + po)
    got(encb.at[4 + ppo], ENC + 8)
    transpose(4 + ppo)
    got(encb.at[ppo], ENC + 9)
    transpose(ppo)

    tl = (((0,), (0,)), ((), ()))
    nt = (((1,), (1,)), ((), ()))

    def attend(i, slot):
        @pl.loop(0, 4)
        def _(t):
            project(2 * (1 - yh), i + 4 * t)

        units = []
        for own in (0, 1):
            head = (yl if own else 1 - yl) * 4 + i
            kc = pl.ds(pl.multiple_of(head * HD, HD), HD)
            vc = pl.ds(pl.multiple_of(INNER + head * HD, HD), HD)
            for m in range(4):
                units.append((own, kc, vc, m))
        raws, pgs = [], []
        for own, kc, vc, m in units:
            raws.append(lax.dot_general(qb[m, :, kc], kv[m, :, kc], nt, preferred_element_type=F32))
            pgs.append(lax.dot_general(gb[m, :, kc], kv[m, :, vc], nt, preferred_element_type=F32))
        raw = jnp.concatenate(raws, axis=0)
        pg = jnp.concatenate(pgs, axis=0)
        e = jnp.exp(raw - jnp.max(raw, axis=-1, keepdims=True))
        prob = e / jnp.sum(e, axis=-1, keepdims=True)
        total = jnp.sum(prob * pg, axis=-1, keepdims=True)
        score = (prob * (pg - total)).astype(BF)
        low = prob.astype(BF)
        for n, (own, kc, vc, m) in enumerate(units):
            s_n, p_n = score[n * Q:(n + 1) * Q], low[n * Q:(n + 1) * Q]
            gqb[m, :, kc] = jnp.dot(s_n, kv[m, :, kc], preferred_element_type=F32).astype(BF)
            kg = lax.dot_general(s_n, qb[m, :, kc], tl, preferred_element_type=F32).astype(BF)
            vg = lax.dot_general(p_n, gb[m, :, kc], tl, preferred_element_type=F32).astype(BF)
            kv[m, :, kc] = kg
            kv[m, :, vc] = vg
            if own:
                rhs[slot, m * LEN:(m + 1) * LEN, 0:HD] = kg
                rhs[slot, m * LEN:(m + 1) * LEN, HD:2 * HD] = vg
            else:
                sco[i, 0, m] = s_n
                sco[i, 1, m] = p_n
        send(sco.at[i], sci.at[i], SC + i, near)

    def weight(i, slot):
        got(sci.at[i], SC + i)
        got(qgn.at[i, 0], QG + 2 * i)
        got(qgn.at[i, 1], QG + 2 * i + 1)
        for m in range(4):
            kg = lax.dot_general(sci[i, 0, m], qgn[i, 0, m], tl, preferred_element_type=F32)
            vg = lax.dot_general(sci[i, 1, m], qgn[i, 1, m], tl, preferred_element_type=F32)
            rhs[slot, 512 + m * LEN:512 + (m + 1) * LEN, 0:HD] = kg.astype(BF)
            rhs[slot, 512 + m * LEN:512 + (m + 1) * LEN, HD:2 * HD] = vg.astype(BF)

        @pl.loop(0, 4)
        def _(xp):
            rows = pl.ds(pl.multiple_of(xp * 512, 512), 512)
            for half in (0, 1):
                out = jnp.dot(enct[rows, :], rhs[slot, :, half * HD:(half + 1) * HD],
                              preferred_element_type=F32).astype(BF)
                for yy in range(2):
                    for zz in range(4):
                        piece = out[yy * 256 + zz * 64:yy * 256 + zz * 64 + 64]
                        if half == 0:
                            part[i, 0, xp, zz * 128 + yy * 64:zz * 128 + yy * 64 + 64] = piece
                        else:
                            at = pl.multiple_of(xp * 128 + yy * 64, 64)
                            part[i, 1, zz, pl.ds(at, 64)] = piece

    first = (x, z)
    second = (z, x)

    hi_rows, lo_rows = pl.ds(0, 256), pl.ds(256, 256)

    def alpha(i):
        for half in (0, 1):
            a, sem = first[half], P1 + (2 * i + half) * 6
            up, down, across = lax.rem(a + 1, 4), lax.rem(a + 3, 4), lax.rem(a + 2, 4)
            send(part.at[i, half, across, hi_rows], f1.at[i, half, 0], sem, peer(half, 1))
            send(part.at[i, half, across, lo_rows], f1.at[i, half, 1], sem + 1, peer(half, 3))
            send(part.at[i, half, up, lo_rows], r1.at[i, half, 0, lo_rows], sem + 2, peer(half, 1))
            send(part.at[i, half, down, hi_rows], r1.at[i, half, 1, hi_rows], sem + 3, peer(half, 3))

    def beta(i):
        for half in (0, 1):
            a, sem = first[half], P1 + (2 * i + half) * 6
            for way, rows, k in ((0, hi_rows, 1), (1, lo_rows, 3)):
                got(f1.at[i, half, way], sem + way)
                block = lax.rem(a + k, 4)

                @pl.loop(0, 4)
                def _(b):
                    src = pl.ds(pl.multiple_of(b * 64, 64), 64)
                    dst = pl.ds(pl.multiple_of(way * 256 + b * 64, 64), 64)
                    acc = part[i, half, block, dst].astype(F32) + f1[i, half, way, src].astype(F32)
                    part[i, half, block, dst] = acc.astype(BF)

                send(part.at[i, half, block, rows], r1.at[i, half, way, rows], sem + 4 + way,
                     peer(half, k))

    def reduce1(i):
        for half in (0, 1):
            a, sem = first[half], P1 + (2 * i + half) * 6
            got(r1.at[i, half, 0, lo_rows], sem + 2)
            got(r1.at[i, half, 1, hi_rows], sem + 3)
            got(r1.at[i, half, 0, hi_rows], sem + 4)
            got(r1.at[i, half, 1, lo_rows], sem + 5)

            @pl.loop(0, 8)
            def _(b):
                rows = pl.ds(pl.multiple_of(b * 64, 64), 64)
                acc = part[i, half, a, rows].astype(F32)
                for k in range(2):
                    acc += r1[i, half, k, rows].astype(F32)
                part[i, half, a, rows] = acc.astype(BF)

            for k in (1, 2, 3):
                rows = pl.ds(pl.multiple_of(lax.rem(second[half] + k, 4) * 128, 128), 128)
                send(part.at[i, half, a, rows], r2.at[i, half, k - 1],
                     P2 + (2 * i + half) * 3 + k - 1, peer(1 - half, k))

    def reduce2(i):
        for half in (0, 1):
            a = first[half]
            for k in (1, 2, 3):
                got(r2.at[i, half, k - 1], P2 + (2 * i + half) * 3 + k - 1)

            def total(which):
                at = pl.ds(pl.multiple_of(second[half] * 128 + which * 64, 64), 64)
                rows = pl.ds(pl.multiple_of(which * 64, 64), 64)
                acc = part[i, half, a, at].astype(F32)
                for k in range(3):
                    acc += r2[i, half, k, rows].astype(F32)
                return acc

            x3[i, half] = total(1 - yl).astype(BF)
            cols = pl.ds(pl.multiple_of(half * INNER + (yl * 4 + i) * HD, HD), HD)
            send(x3.at[i, half], outb.at[:, cols], P3 + 2 * i + half, near)
            outb[:, cols] = total(yl).astype(BF)

    def finish(i):
        for half in (0, 1):
            cols = pl.ds(pl.multiple_of(half * INNER + ((1 - yl) * 4 + i) * HD, HD), HD)
            got(outb.at[:, cols], P3 + 2 * i + half)

    def enc_term(piece):
        @pl.loop(0, 2)
        def _(t):
            cols = pl.ds(pl.multiple_of(piece * 512 + t * 256, 256), 256)
            out = lax.dot_general(kv[...].reshape(512, 2 * INNER), w[cols, :], nt,
                                  preferred_element_type=F32).reshape(4, LEN, 256)
            for u in (0, 1):
                ek[u, :, cols] = jnp.where(c == 0, out[2 * u], out[2 * u + 1])
                es[u, :, cols] = jnp.where(c == 0, out[2 * u + 1], out[2 * u]).astype(BF)

        cols = pl.ds(piece * 512, 512)
        send(es.at[:, :, cols], er.at[:, :, cols], E1 + piece, core)

    def enc_pair(piece):
        cols = pl.ds(piece * 512, 512)
        got(er.at[:, :, cols], E1 + piece)
        ys[:, cols] = (ek[1 - yh, :, cols] + er[1 - yh, :, cols].astype(F32)).astype(BF)
        send(ys.at[:, cols], yr.at[:, cols], E2 + piece, partner)
        ek[yh, :, cols] = ek[yh, :, cols] + er[yh, :, cols].astype(F32)

    def enc_last(piece):
        cols = pl.ds(piece * 512, 512)
        got(yr.at[:, cols], E2 + piece)
        ek[yh, :, cols] = ek[yh, :, cols] + yr[:, cols].astype(F32)

    attend(0, 0)
    attend(1, 1)
    weight(0, 0)
    alpha(0)
    attend(2, 0)
    weight(1, 1)
    alpha(1)
    beta(0)
    attend(3, 1)
    out_q = pltpu.make_async_copy(gqb, gq_hbm.at[0], lsem.at[3])
    out_q.start()
    weight(2, 0)
    alpha(2)
    beta(1)
    weight(3, 1)
    alpha(3)
    enc_term(0)
    reduce1(0)
    beta(2)
    enc_term(1)
    beta(3)
    enc_pair(0)
    enc_term(2)
    reduce1(1)
    enc_pair(1)
    enc_term(3)
    enc_pair(2)
    reduce2(0)
    enc_pair(3)
    reduce1(2)
    reduce2(1)
    for piece in range(4):
        enc_last(piece)
    out_e = pltpu.make_async_copy(ek.at[yh], genc_hbm.at[0], lsem.at[4])
    out_e.start()
    reduce1(3)
    reduce2(2)
    reduce2(3)
    for i in range(4):
        finish(i)
    out_w = pltpu.make_async_copy(outb, gkv_hbm.at[0], lsem.at[5])
    out_w.start()
    for cp in sends:
        cp.wait_send()
    out_q.wait()
    out_e.wait()
    out_w.wait()


def hand_over(gkv, genc, gq, gkv_out, genc_out, gq_out, low, wide, enc, query, isem, osem):
    loads = [pltpu.make_async_copy(src.at[0], dst, isem.at[n])
             for n, (src, dst) in enumerate(((gkv, low), (genc, enc), (gq, query)))]
    stores = [pltpu.make_async_copy(src, dst.at[0], osem.at[n])
              for n, (src, dst) in enumerate(((wide, gkv_out), (enc, genc_out), (query, gq_out)))]
    for cp in loads:
        cp.start()
    for n, (load, store) in enumerate(zip(loads, stores)):
        load.wait()
        if n == 0:
            @pl.loop(0, 8)
            def _(b):
                cols = pl.ds(pl.multiple_of(b * 512, 512), 512)
                wide[:, cols] = low[:, cols].astype(F32)
        store.start()
    for cp in stores:
        cp.wait()


def per_device(enc_out, kv_weight, queries, out_grad):
    anywhere = pl.BlockSpec(memory_space=pl.ANY)
    vm = pltpu.VMEM
    gkv, genc, gq = pl.pallas_call(
        body,
        out_shape=(
            jax.ShapeDtypeStruct((1, 64, 2 * INNER), BF),
            jax.ShapeDtypeStruct((1, LEN, D), F32),
            jax.ShapeDtypeStruct((1, 4, Q, INNER), BF),
        ),
        in_specs=[anywhere] * 4,
        out_specs=(anywhere,) * 3,
        scratch_shapes=[
            vm((D, 2 * INNER), BF),
            vm((8, LEN, D), BF),
            vm((D, 8 * LEN), BF),
            vm((4, LEN, 2 * INNER), BF),
            vm((4, Q, INNER), BF),
            vm((4, Q, INNER), BF),
            vm((4, 2, 4, Q, HD), BF),
            vm((4, Q, INNER), BF),
            vm((4, 2, 4, Q, LEN), BF),
            vm((4, 2, 4, Q, LEN), BF),
            vm((2, 8 * LEN, 2 * HD), BF),
            vm((4, 2, 4, 512, HD), BF),
            vm((4, 2, 2, 256, HD), BF),
            vm((4, 2, 2, 512, HD), BF),
            vm((4, 2, 3, 128, HD), BF),
            vm((4, 2, 64, HD), BF),
            vm((64, 2 * INNER), BF),
            vm((2, LEN, D), F32),
            vm((2, LEN, D), BF),
            vm((2, LEN, D), BF),
            vm((LEN, D), BF),
            vm((LEN, D), BF),
            pltpu.SemaphoreType.DMA((6,)),
            pltpu.SemaphoreType.DMA((16,)),
            pltpu.SemaphoreType.DMA((NSEM,)),
            pltpu.SemaphoreType.DMA((NSEM,)),
        ],
        compiler_params=pltpu.CompilerParams(
            collective_id=0, has_side_effects=True, vmem_limit_bytes=62 * 1024 * 1024),
        name="kv_backward",
    )(enc_out, kv_weight, queries, out_grad)
    return pl.pallas_call(
        hand_over,
        out_shape=(
            jax.ShapeDtypeStruct((1, 64, 2 * INNER), F32),
            jax.ShapeDtypeStruct((1, LEN, D), F32),
            jax.ShapeDtypeStruct((1, 4, Q, INNER), BF),
        ),
        in_specs=[anywhere] * 3,
        out_specs=(anywhere,) * 3,
        scratch_shapes=[
            vm((64, 2 * INNER), BF),
            vm((64, 2 * INNER), F32),
            vm((LEN, D), F32),
            vm((4, Q, INNER), BF),
            pltpu.SemaphoreType.DMA((3,)),
            pltpu.SemaphoreType.DMA((3,)),
        ],
        compiler_params=pltpu.CompilerParams(vmem_limit_bytes=16 * 1024 * 1024),
        name="hand_over",
    )(gkv, genc, gq)


def solution(mesh):
    placed = (
        P("pipe", "dp", None),
        P("pipe", None, None),
        P("pipe", None, "dp", None),
        P("pipe", None, "dp", None),
    )
    return jax.shard_map(
        per_device,
        mesh=mesh,
        in_specs=placed,
        out_specs=(P("pipe", "dp", None), P("pipe", "dp", None), P("pipe", None, "dp", None)),
        check_vma=False,
    )
```

```python
import jax
import jax.numpy as jnp
from jax import lax
from jax.experimental import pallas as pl
from jax.experimental.pallas import tpu as pltpu
from jax.sharding import PartitionSpec as P

HD = 256
INNER = 2048
D = 2048
LEN = 128
Q = 32
BF = jnp.bfloat16
F32 = jnp.float32
MESH = pl.DeviceIdType.MESH

ENC, QG, SC, P1, P2, P3, E1, E2, NSEM = 0, 10, 18, 22, 70, 94, 102, 106, 110


def body(enc_hbm, w_hbm, q_hbm, g_hbm, gkv_hbm, genc_hbm, gq_hbm,
         w, encb, enct, kv, qb, gb, qgn, gqb, sco, sci, rhs, part, f1, r1, r2, x3, outb,
         ek, es, er, ys, yr, lsem, wsem, ssem, rsem):
    p = lax.axis_index("pipe")
    d = lax.axis_index("dp")
    yh, c = p // 2, p % 2
    x, yl, z = d // 8, (d // 4) % 2, d % 4
    po = 2 * yh + 1 - c
    pp = 2 * (1 - yh) + c
    ppo = 2 * (1 - yh) + 1 - c
    dn = x * 8 + (1 - yl) * 4 + z
    core, partner, near, far = (po, d), (pp, d), (p, dn), (pp, dn)

    def peer(half_axis, k):
        if half_axis == 0:
            return (p, lax.rem(x + k, 4) * 8 + yl * 4 + z)
        return (p, x * 8 + yl * 4 + lax.rem(z + k, 4))

    def rc(src, dst, idx, dev):
        return pltpu.make_async_remote_copy(
            src_ref=src, dst_ref=dst, send_sem=ssem.at[idx], recv_sem=rsem.at[idx],
            device_id=dev, device_id_type=MESH)

    def got(dst, idx):
        rc(dst, dst, idx, core).wait_recv()

    def w_copy(j):
        cols = pl.ds(pl.multiple_of(j * 256, 256), 256)
        return pltpu.make_async_copy(w_hbm.at[0, :, cols], w.at[:, cols], wsem.at[j])

    own_enc = pltpu.make_async_copy(enc_hbm.at[0], encb.at[p], lsem.at[0])
    own_q = pltpu.make_async_copy(q_hbm.at[0], qb, lsem.at[1])
    own_g = pltpu.make_async_copy(g_hbm.at[0], gb, lsem.at[2])
    own_enc.start()

    @pl.loop(0, 16)
    def _(j):
        w_copy(j).start()

    own_q.start()
    own_g.start()

    barrier = pltpu.get_barrier_semaphore()
    others = [core, partner, near, far] + [peer(h, k) for h in (0, 1) for k in (1, 2, 3)]
    for dev in others:
        pl.semaphore_signal(barrier, inc=1, device_id=dev, device_id_type=MESH)
    pl.semaphore_wait(barrier, len(others))

    sends = []

    def send(src, dst, idx, dev):
        cp = rc(src, dst, idx, dev)
        cp.start()
        sends.append(cp)

    top, low_rows = pl.ds(0, 64), pl.ds(64, 64)
    send(enc_hbm.at[0], encb.at[p], ENC + 0, core)
    send(enc_hbm.at[0, top], encb.at[4 + p, top], ENC + 1, near)
    send(enc_hbm.at[0, low_rows], encb.at[4 + p, low_rows], ENC + 3, far)

    def project(first, j):
        cols = pl.ds(pl.multiple_of(j * 256, 256), 256)
        rows = encb[pl.ds(first, 2)].reshape(256, D)
        out = jnp.dot(rows, w[:, cols], preferred_element_type=F32)
        kv[pl.ds(first, 2), :, cols] = out.astype(BF).reshape(2, LEN, 256)

    def transpose(slot):
        cols = pl.ds(pl.multiple_of(slot * LEN, LEN), LEN)

        @pl.loop(0, 8)
        def _(b):
            rows = pl.ds(pl.multiple_of(b * 256, 256), 256)
            enct[rows, cols] = encb[slot, :, rows].T

    own_enc.wait()
    got(encb.at[po], ENC + 0)

    def local_kv(lo, hi):
        @pl.loop(lo, hi)
        def _(j):
            w_copy(j).wait()
            project(2 * yh, j)

    def send_factors(i):
        cols = pl.ds(pl.multiple_of((1 - yl) * 1024 + i * 256, 256), 256)
        send(qb.at[:, :, cols], qgn.at[i, 0], QG + 2 * i, near)
        send(gb.at[:, :, cols], qgn.at[i, 1], QG + 2 * i + 1, near)

    local_kv(0, 4)
    got(encb.at[4 + p, top], ENC + 1)
    send(encb.at[4 + p, top], encb.at[p, top], ENC + 5, far)
    got(encb.at[4 + pp, low_rows], ENC + 3)
    send(encb.at[4 + pp, low_rows], encb.at[pp, low_rows], ENC + 6, near)
    own_q.wait()
    own_g.wait()
    local_kv(4, 13)
    got(encb.at[pp, top], ENC + 5)
    got(encb.at[pp, low_rows], ENC + 6)
    send(encb.at[pp], encb.at[pp], ENC + 9, core)
    send(enc_hbm.at[0, low_rows], encb.at[4 + p, low_rows], ENC + 2, near)
    send(enc_hbm.at[0, top], encb.at[4 + p, top], ENC + 4, far)
    send_factors(0)
    local_kv(13, 16)
    transpose(p)
    got(encb.at[ppo], ENC + 9)

    tl = (((0,), (0,)), ((), ()))
    nt = (((1,), (1,)), ((), ()))

    def rest_kv(i):
        @pl.loop(0, 4)
        def _(t):
            project(2 * (1 - yh), i + 4 * t)

    def attend(i, slot):
        units = []
        for own in (0, 1):
            head = (yl if own else 1 - yl) * 4 + i
            kc = pl.ds(pl.multiple_of(head * HD, HD), HD)
            vc = pl.ds(pl.multiple_of(INNER + head * HD, HD), HD)
            for m in range(4):
                units.append((own, kc, vc, m))
        raws, pgs = [], []
        for own, kc, vc, m in units:
            raws.append(lax.dot_general(qb[m, :, kc], kv[m, :, kc], nt, preferred_element_type=F32))
            pgs.append(lax.dot_general(gb[m, :, kc], kv[m, :, vc], nt, preferred_element_type=F32))
        raw = jnp.concatenate(raws, axis=0)
        pg = jnp.concatenate(pgs, axis=0)
        e = jnp.exp(raw - jnp.max(raw, axis=-1, keepdims=True))
        prob = e / jnp.sum(e, axis=-1, keepdims=True)
        total = jnp.sum(prob * pg, axis=-1, keepdims=True)
        score = (prob * (pg - total)).astype(BF)
        low = prob.astype(BF)
        for n, (own, kc, vc, m) in enumerate(units):
            s_n, p_n = score[n * Q:(n + 1) * Q], low[n * Q:(n + 1) * Q]
            gqb[m, :, kc] = jnp.dot(s_n, kv[m, :, kc], preferred_element_type=F32).astype(BF)
            kg = lax.dot_general(s_n, qb[m, :, kc], tl, preferred_element_type=F32).astype(BF)
            vg = lax.dot_general(p_n, gb[m, :, kc], tl, preferred_element_type=F32).astype(BF)
            kv[m, :, kc] = kg
            kv[m, :, vc] = vg
            if own:
                rhs[slot, m * LEN:(m + 1) * LEN, 0:HD] = kg
                rhs[slot, m * LEN:(m + 1) * LEN, HD:2 * HD] = vg
            else:
                sco[i, 0, m] = s_n
                sco[i, 1, m] = p_n
        send(sco.at[i], sci.at[i], SC + i, near)

    def weight(i, slot):
        got(sci.at[i], SC + i)
        got(qgn.at[i, 0], QG + 2 * i)
        got(qgn.at[i, 1], QG + 2 * i + 1)
        for m in range(4):
            kg = lax.dot_general(sci[i, 0, m], qgn[i, 0, m], tl, preferred_element_type=F32)
            vg = lax.dot_general(sci[i, 1, m], qgn[i, 1, m], tl, preferred_element_type=F32)
            rhs[slot, 512 + m * LEN:512 + (m + 1) * LEN, 0:HD] = kg.astype(BF)
            rhs[slot, 512 + m * LEN:512 + (m + 1) * LEN, HD:2 * HD] = vg.astype(BF)

        for half in (0, 1):
            @pl.loop(0, 4)
            def _(xp):
                rows = pl.ds(pl.multiple_of(xp * 512, 512), 512)
                out = jnp.dot(enct[rows, :], rhs[slot, :, half * HD:(half + 1) * HD],
                              preferred_element_type=F32).astype(BF)
                for yy in range(2):
                    for zz in range(4):
                        piece = out[yy * 256 + zz * 64:yy * 256 + zz * 64 + 64]
                        if half == 0:
                            part[i, 0, xp, zz * 128 + yy * 64:zz * 128 + yy * 64 + 64] = piece
                        else:
                            at = pl.multiple_of(xp * 128 + yy * 64, 64)
                            part[i, 1, zz, pl.ds(at, 64)] = piece

            alpha(i, half)

    first = (x, z)
    second = (z, x)

    hi_rows, lo_rows = pl.ds(0, 256), pl.ds(256, 256)

    def alpha(i, half):
        a, sem = first[half], P1 + (2 * i + half) * 6
        across = lax.rem(a + 2, 4)
        send(part.at[i, half, across, hi_rows], f1.at[i, half, 0], sem, peer(half, 1))
        send(part.at[i, half, across, lo_rows], f1.at[i, half, 1], sem + 1, peer(half, 3))

    def direct(i):
        for half in (0, 1):
            a, sem = first[half], P1 + (2 * i + half) * 6
            up, down = lax.rem(a + 1, 4), lax.rem(a + 3, 4)
            send(part.at[i, half, up, lo_rows], r1.at[i, half, 0, lo_rows], sem + 2, peer(half, 1))
            send(part.at[i, half, down, hi_rows], r1.at[i, half, 1, hi_rows], sem + 3, peer(half, 3))

    def beta(i):
        for half in (0, 1):
            a, sem = first[half], P1 + (2 * i + half) * 6
            for way, rows, k in ((0, hi_rows, 1), (1, lo_rows, 3)):
                got(f1.at[i, half, way], sem + way)
                block = lax.rem(a + k, 4)

                @pl.loop(0, 4)
                def _(b):
                    src = pl.ds(pl.multiple_of(b * 64, 64), 64)
                    dst = pl.ds(pl.multiple_of(way * 256 + b * 64, 64), 64)
                    acc = part[i, half, block, dst].astype(F32) + f1[i, half, way, src].astype(F32)
                    part[i, half, block, dst] = acc.astype(BF)

                send(part.at[i, half, block, rows], r1.at[i, half, way, rows], sem + 4 + way,
                     peer(half, k))

    def reduce1(i):
        for half in (0, 1):
            a, sem = first[half], P1 + (2 * i + half) * 6
            got(r1.at[i, half, 0, lo_rows], sem + 2)
            got(r1.at[i, half, 1, hi_rows], sem + 3)
            got(r1.at[i, half, 0, hi_rows], sem + 4)
            got(r1.at[i, half, 1, lo_rows], sem + 5)

            @pl.loop(0, 8)
            def _(b):
                rows = pl.ds(pl.multiple_of(b * 64, 64), 64)
                acc = part[i, half, a, rows].astype(F32)
                for k in range(2):
                    acc += r1[i, half, k, rows].astype(F32)
                part[i, half, a, rows] = acc.astype(BF)

            for k in (1, 2, 3):
                rows = pl.ds(pl.multiple_of(lax.rem(second[half] + k, 4) * 128, 128), 128)
                send(part.at[i, half, a, rows], r2.at[i, half, k - 1],
                     P2 + (2 * i + half) * 3 + k - 1, peer(1 - half, k))

    def reduce2(i):
        for half in (0, 1):
            a = first[half]
            for k in (1, 2, 3):
                got(r2.at[i, half, k - 1], P2 + (2 * i + half) * 3 + k - 1)

            def total(which):
                at = pl.ds(pl.multiple_of(second[half] * 128 + which * 64, 64), 64)
                rows = pl.ds(pl.multiple_of(which * 64, 64), 64)
                acc = part[i, half, a, at].astype(F32)
                for k in range(3):
                    acc += r2[i, half, k, rows].astype(F32)
                return acc

            x3[i, half] = total(1 - yl).astype(BF)
            cols = pl.ds(pl.multiple_of(half * INNER + (yl * 4 + i) * HD, HD), HD)
            send(x3.at[i, half], outb.at[:, cols], P3 + 2 * i + half, near)
            outb[:, cols] = total(yl).astype(BF)

    def finish(i):
        for half in (0, 1):
            cols = pl.ds(pl.multiple_of(half * INNER + ((1 - yl) * 4 + i) * HD, HD), HD)
            got(outb.at[:, cols], P3 + 2 * i + half)

    def enc_term(piece):
        @pl.loop(0, 2)
        def _(t):
            cols = pl.ds(pl.multiple_of(piece * 512 + t * 256, 256), 256)
            out = lax.dot_general(kv[...].reshape(512, 2 * INNER), w[cols, :], nt,
                                  preferred_element_type=F32).reshape(4, LEN, 256)
            for u in (0, 1):
                ek[u, :, cols] = jnp.where(c == 0, out[2 * u], out[2 * u + 1])
                es[u, :, cols] = jnp.where(c == 0, out[2 * u + 1], out[2 * u]).astype(BF)

        cols = pl.ds(piece * 512, 512)
        send(es.at[:, :, cols], er.at[:, :, cols], E1 + piece, core)

    def enc_pair(piece):
        cols = pl.ds(piece * 512, 512)
        got(er.at[:, :, cols], E1 + piece)
        ys[:, cols] = (ek[1 - yh, :, cols] + er[1 - yh, :, cols].astype(F32)).astype(BF)
        send(ys.at[:, cols], yr.at[:, cols], E2 + piece, partner)
        ek[yh, :, cols] = ek[yh, :, cols] + er[yh, :, cols].astype(F32)

    def enc_last(piece):
        cols = pl.ds(piece * 512, 512)
        got(yr.at[:, cols], E2 + piece)
        ek[yh, :, cols] = ek[yh, :, cols] + yr[:, cols].astype(F32)

    rest_kv(0)
    attend(0, 0)
    transpose(po)
    transpose(pp)
    transpose(ppo)
    rest_kv(1)
    got(encb.at[4 + p, low_rows], ENC + 2)
    send(encb.at[4 + p], encb.at[4 + p], ENC + 7, core)
    got(encb.at[4 + pp, top], ENC + 4)
    send(encb.at[4 + pp], encb.at[4 + pp], ENC + 8, core)
    send_factors(1)
    transpose(4 + p)
    transpose(4 + pp)
    got(encb.at[4 + po], ENC + 7)
    transpose(4 + po)
    got(encb.at[4 + ppo], ENC + 8)
    transpose(4 + ppo)
    weight(0, 0)
    attend(1, 1)
    direct(0)
    send_factors(2)
    rest_kv(2)
    beta(0)
    weight(1, 1)
    attend(2, 0)
    direct(1)
    send_factors(3)
    rest_kv(3)
    beta(1)
    weight(2, 0)
    attend(3, 1)
    direct(2)
    out_q = pltpu.make_async_copy(gqb, gq_hbm.at[0], lsem.at[3])
    out_q.start()
    reduce1(0)
    beta(2)
    weight(3, 1)
    direct(3)
    enc_term(0)
    reduce1(1)
    enc_term(1)
    beta(3)
    enc_pair(0)
    reduce2(0)
    enc_term(2)
    enc_pair(1)
    reduce1(2)
    enc_term(3)
    enc_pair(2)
    reduce2(1)
    reduce1(3)
    enc_pair(3)
    reduce2(2)
    reduce2(3)
    for piece in range(4):
        enc_last(piece)
    out_e = pltpu.make_async_copy(ek.at[yh], genc_hbm.at[0], lsem.at[4])
    out_e.start()
    for i in range(4):
        finish(i)
    out_w = pltpu.make_async_copy(outb, gkv_hbm.at[0], lsem.at[5])
    out_w.start()
    for cp in sends:
        cp.wait_send()
    out_q.wait()
    out_e.wait()
    out_w.wait()


def hand_over(gkv, genc, gq, gkv_out, genc_out, gq_out, low, wide, enc, query, isem, osem):
    loads = [pltpu.make_async_copy(src.at[0], dst, isem.at[n])
             for n, (src, dst) in enumerate(((gkv, low), (genc, enc), (gq, query)))]
    stores = [pltpu.make_async_copy(src, dst.at[0], osem.at[n])
              for n, (src, dst) in enumerate(((wide, gkv_out), (enc, genc_out), (query, gq_out)))]
    for cp in loads:
        cp.start()
    for n, (load, store) in enumerate(zip(loads, stores)):
        load.wait()
        if n == 0:
            @pl.loop(0, 8)
            def _(b):
                cols = pl.ds(pl.multiple_of(b * 512, 512), 512)
                wide[:, cols] = low[:, cols].astype(F32)
        store.start()
    for cp in stores:
        cp.wait()


def per_device(enc_out, kv_weight, queries, out_grad):
    anywhere = pl.BlockSpec(memory_space=pl.ANY)
    vm = pltpu.VMEM
    gkv, genc, gq = pl.pallas_call(
        body,
        out_shape=(
            jax.ShapeDtypeStruct((1, 64, 2 * INNER), BF),
            jax.ShapeDtypeStruct((1, LEN, D), F32),
            jax.ShapeDtypeStruct((1, 4, Q, INNER), BF),
        ),
        in_specs=[anywhere] * 4,
        out_specs=(anywhere,) * 3,
        scratch_shapes=[
            vm((D, 2 * INNER), BF),
            vm((8, LEN, D), BF),
            vm((D, 8 * LEN), BF),
            vm((4, LEN, 2 * INNER), BF),
            vm((4, Q, INNER), BF),
            vm((4, Q, INNER), BF),
            vm((4, 2, 4, Q, HD), BF),
            vm((4, Q, INNER), BF),
            vm((4, 2, 4, Q, LEN), BF),
            vm((4, 2, 4, Q, LEN), BF),
            vm((2, 8 * LEN, 2 * HD), BF),
            vm((4, 2, 4, 512, HD), BF),
            vm((4, 2, 2, 256, HD), BF),
            vm((4, 2, 2, 512, HD), BF),
            vm((4, 2, 3, 128, HD), BF),
            vm((4, 2, 64, HD), BF),
            vm((64, 2 * INNER), BF),
            vm((2, LEN, D), F32),
            vm((2, LEN, D), BF),
            vm((2, LEN, D), BF),
            vm((LEN, D), BF),
            vm((LEN, D), BF),
            pltpu.SemaphoreType.DMA((6,)),
            pltpu.SemaphoreType.DMA((16,)),
            pltpu.SemaphoreType.DMA((NSEM,)),
            pltpu.SemaphoreType.DMA((NSEM,)),
        ],
        compiler_params=pltpu.CompilerParams(
            collective_id=0, has_side_effects=True, vmem_limit_bytes=62 * 1024 * 1024),
        name="kv_backward",
    )(enc_out, kv_weight, queries, out_grad)
    return pl.pallas_call(
        hand_over,
        out_shape=(
            jax.ShapeDtypeStruct((1, 64, 2 * INNER), F32),
            jax.ShapeDtypeStruct((1, LEN, D), F32),
            jax.ShapeDtypeStruct((1, 4, Q, INNER), BF),
        ),
        in_specs=[anywhere] * 3,
        out_specs=(anywhere,) * 3,
        scratch_shapes=[
            vm((64, 2 * INNER), BF),
            vm((64, 2 * INNER), F32),
            vm((LEN, D), F32),
            vm((4, Q, INNER), BF),
            pltpu.SemaphoreType.DMA((3,)),
            pltpu.SemaphoreType.DMA((3,)),
        ],
        compiler_params=pltpu.CompilerParams(vmem_limit_bytes=16 * 1024 * 1024),
        name="hand_over",
    )(gkv, genc, gq)


def solution(mesh):
    placed = (
        P("pipe", "dp", None),
        P("pipe", None, None),
        P("pipe", None, "dp", None),
        P("pipe", None, "dp", None),
    )
    return jax.shard_map(
        per_device,
        mesh=mesh,
        in_specs=placed,
        out_specs=(P("pipe", "dp", None), P("pipe", "dp", None), P("pipe", None, "dp", None)),
        check_vma=False,
    )
```

```python
import jax
import jax.numpy as jnp
from jax import lax
from jax.experimental import pallas as pl
from jax.experimental.pallas import tpu as pltpu
from jax.sharding import PartitionSpec as P

HD = 256
INNER = 2048
D = 2048
LEN = 128
Q = 32
BF = jnp.bfloat16
F32 = jnp.float32
MESH = pl.DeviceIdType.MESH

ENC, QG, SC, P1, P2, P3, E1, E2, NSEM = 0, 10, 18, 22, 70, 94, 102, 106, 110


def body(enc_hbm, w_hbm, q_hbm, g_hbm, gkv_hbm, genc_hbm, gq_hbm,
         w, encb, enct, kv, qb, gb, qgn, gqb, sco, sci, rhs, part, f1, r1, r2, x3, outb,
         ek, es, er, ys, yr, lsem, wsem, ssem, rsem):
    p = lax.axis_index("pipe")
    d = lax.axis_index("dp")
    yh, c = p // 2, p % 2
    x, yl, z = d // 8, (d // 4) % 2, d % 4
    po = 2 * yh + 1 - c
    pp = 2 * (1 - yh) + c
    ppo = 2 * (1 - yh) + 1 - c
    dn = x * 8 + (1 - yl) * 4 + z
    core, partner, near, far = (po, d), (pp, d), (p, dn), (pp, dn)

    def peer(half_axis, k):
        if half_axis == 0:
            return (p, lax.rem(x + k, 4) * 8 + yl * 4 + z)
        return (p, x * 8 + yl * 4 + lax.rem(z + k, 4))

    def rc(src, dst, idx, dev):
        return pltpu.make_async_remote_copy(
            src_ref=src, dst_ref=dst, send_sem=ssem.at[idx], recv_sem=rsem.at[idx],
            device_id=dev, device_id_type=MESH)

    def got(dst, idx):
        rc(dst, dst, idx, core).wait_recv()

    def w_copy(j):
        cols = pl.ds(pl.multiple_of(j * 256, 256), 256)
        return pltpu.make_async_copy(w_hbm.at[0, :, cols], w.at[:, cols], wsem.at[j])

    own_enc = pltpu.make_async_copy(enc_hbm.at[0], encb.at[p], lsem.at[0])
    own_q = pltpu.make_async_copy(q_hbm.at[0], qb, lsem.at[1])
    own_g = pltpu.make_async_copy(g_hbm.at[0], gb, lsem.at[2])
    own_enc.start()

    @pl.loop(0, 16)
    def _(j):
        w_copy(j).start()

    own_q.start()
    own_g.start()

    barrier = pltpu.get_barrier_semaphore()
    others = [core, partner, near, far] + [peer(h, k) for h in (0, 1) for k in (1, 2, 3)]
    for dev in others:
        pl.semaphore_signal(barrier, inc=1, device_id=dev, device_id_type=MESH)
    pl.semaphore_wait(barrier, len(others))

    sends = []

    def send(src, dst, idx, dev):
        cp = rc(src, dst, idx, dev)
        cp.start()
        sends.append(cp)

    top, low_rows = pl.ds(0, 64), pl.ds(64, 64)
    send(enc_hbm.at[0], encb.at[p], ENC + 0, core)
    send(enc_hbm.at[0, top], encb.at[4 + p, top], ENC + 1, near)
    send(enc_hbm.at[0, low_rows], encb.at[4 + p, low_rows], ENC + 3, far)

    def project(first, j):
        cols = pl.ds(pl.multiple_of(j * 256, 256), 256)
        rows = encb[pl.ds(first, 2)].reshape(256, D)
        out = jnp.dot(rows, w[:, cols], preferred_element_type=F32)
        kv[pl.ds(first, 2), :, cols] = out.astype(BF).reshape(2, LEN, 256)

    def transpose(slot):
        cols = pl.ds(pl.multiple_of(slot * LEN, LEN), LEN)

        @pl.loop(0, 8)
        def _(b):
            rows = pl.ds(pl.multiple_of(b * 256, 256), 256)
            enct[rows, cols] = encb[slot, :, rows].T

    own_enc.wait()
    got(encb.at[po], ENC + 0)

    def local_kv(lo, hi):
        @pl.loop(lo, hi)
        def _(j):
            w_copy(j).wait()
            project(2 * yh, j)

    def send_factors(i):
        cols = pl.ds(pl.multiple_of((1 - yl) * 1024 + i * 256, 256), 256)
        send(qb.at[:, :, cols], qgn.at[i, 0], QG + 2 * i, near)
        send(gb.at[:, :, cols], qgn.at[i, 1], QG + 2 * i + 1, near)

    local_kv(0, 4)
    got(encb.at[4 + p, top], ENC + 1)
    send(encb.at[4 + p, top], encb.at[p, top], ENC + 5, far)
    got(encb.at[4 + pp, low_rows], ENC + 3)
    send(encb.at[4 + pp, low_rows], encb.at[pp, low_rows], ENC + 6, near)
    own_q.wait()
    own_g.wait()
    local_kv(4, 13)
    got(encb.at[pp, top], ENC + 5)
    got(encb.at[pp, low_rows], ENC + 6)
    send(encb.at[pp], encb.at[pp], ENC + 9, core)
    send(enc_hbm.at[0, low_rows], encb.at[4 + p, low_rows], ENC + 2, near)
    send(enc_hbm.at[0, top], encb.at[4 + p, top], ENC + 4, far)
    send_factors(0)
    local_kv(13, 16)
    transpose(p)
    got(encb.at[ppo], ENC + 9)

    tl = (((0,), (0,)), ((), ()))
    nt = (((1,), (1,)), ((), ()))

    def rest_kv(i):
        @pl.loop(0, 4)
        def _(t):
            project(2 * (1 - yh), i + 4 * t)

    def attend(i, slot):
        units = []
        for own in (0, 1):
            head = (yl if own else 1 - yl) * 4 + i
            kc = pl.ds(pl.multiple_of(head * HD, HD), HD)
            vc = pl.ds(pl.multiple_of(INNER + head * HD, HD), HD)
            for m in range(4):
                units.append((own, kc, vc, m))
        raws, pgs = [], []
        for own, kc, vc, m in units:
            raws.append(lax.dot_general(qb[m, :, kc], kv[m, :, kc], nt, preferred_element_type=F32))
            pgs.append(lax.dot_general(gb[m, :, kc], kv[m, :, vc], nt, preferred_element_type=F32))
        raw = jnp.concatenate(raws, axis=0)
        pg = jnp.concatenate(pgs, axis=0)
        e = jnp.exp(raw - jnp.max(raw, axis=-1, keepdims=True))
        prob = e / jnp.sum(e, axis=-1, keepdims=True)
        total = jnp.sum(prob * pg, axis=-1, keepdims=True)
        score = (prob * (pg - total)).astype(BF)
        low = prob.astype(BF)
        for n, (own, kc, vc, m) in enumerate(units):
            s_n, p_n = score[n * Q:(n + 1) * Q], low[n * Q:(n + 1) * Q]
            gqb[m, :, kc] = jnp.dot(s_n, kv[m, :, kc], preferred_element_type=F32).astype(BF)
            kg = lax.dot_general(s_n, qb[m, :, kc], tl, preferred_element_type=F32).astype(BF)
            vg = lax.dot_general(p_n, gb[m, :, kc], tl, preferred_element_type=F32).astype(BF)
            kv[m, :, kc] = kg
            kv[m, :, vc] = vg
            if own:
                rhs[slot, m * LEN:(m + 1) * LEN, 0:HD] = kg
                rhs[slot, m * LEN:(m + 1) * LEN, HD:2 * HD] = vg
            else:
                sco[i, 0, m] = s_n
                sco[i, 1, m] = p_n
        send(sco.at[i], sci.at[i], SC + i, near)

    def weight(i, slot):
        got(sci.at[i], SC + i)
        got(qgn.at[i, 0], QG + 2 * i)
        got(qgn.at[i, 1], QG + 2 * i + 1)
        for m in range(4):
            kg = lax.dot_general(sci[i, 0, m], qgn[i, 0, m], tl, preferred_element_type=F32)
            vg = lax.dot_general(sci[i, 1, m], qgn[i, 1, m], tl, preferred_element_type=F32)
            rhs[slot, 512 + m * LEN:512 + (m + 1) * LEN, 0:HD] = kg.astype(BF)
            rhs[slot, 512 + m * LEN:512 + (m + 1) * LEN, HD:2 * HD] = vg.astype(BF)

        for half in (0, 1):
            @pl.loop(0, 4)
            def _(xp):
                rows = pl.ds(pl.multiple_of(xp * 512, 512), 512)
                out = jnp.dot(enct[rows, :], rhs[slot, :, half * HD:(half + 1) * HD],
                              preferred_element_type=F32).astype(BF)
                for yy in range(2):
                    for zz in range(4):
                        piece = out[yy * 256 + zz * 64:yy * 256 + zz * 64 + 64]
                        if half == 0:
                            part[i, 0, xp, zz * 128 + yy * 64:zz * 128 + yy * 64 + 64] = piece
                        else:
                            at = pl.multiple_of(xp * 128 + yy * 64, 64)
                            part[i, 1, zz, pl.ds(at, 64)] = piece

            alpha(i, half)

    first = (x, z)
    second = (z, x)

    hi_rows, lo_rows = pl.ds(0, 256), pl.ds(256, 256)

    def alpha(i, half):
        a, sem = first[half], P1 + (2 * i + half) * 6
        across = lax.rem(a + 2, 4)
        send(part.at[i, half, across, hi_rows], f1.at[i, half, 0], sem, peer(half, 1))
        send(part.at[i, half, across, lo_rows], f1.at[i, half, 1], sem + 1, peer(half, 3))

    def direct(i):
        for half in (0, 1):
            a, sem = first[half], P1 + (2 * i + half) * 6
            up, down = lax.rem(a + 1, 4), lax.rem(a + 3, 4)
            send(part.at[i, half, up, lo_rows], r1.at[i, half, 0, lo_rows], sem + 2, peer(half, 1))
            send(part.at[i, half, down, hi_rows], r1.at[i, half, 1, hi_rows], sem + 3, peer(half, 3))

    def beta(i):
        for half in (0, 1):
            a, sem = first[half], P1 + (2 * i + half) * 6
            for way, rows, k in ((0, hi_rows, 1), (1, lo_rows, 3)):
                got(f1.at[i, half, way], sem + way)
                block = lax.rem(a + k, 4)

                @pl.loop(0, 4)
                def _(b):
                    src = pl.ds(pl.multiple_of(b * 64, 64), 64)
                    dst = pl.ds(pl.multiple_of(way * 256 + b * 64, 64), 64)
                    acc = part[i, half, block, dst].astype(F32) + f1[i, half, way, src].astype(F32)
                    part[i, half, block, dst] = acc.astype(BF)

                send(part.at[i, half, block, rows], r1.at[i, half, way, rows], sem + 4 + way,
                     peer(half, k))

    def reduce1(i):
        for half in (0, 1):
            a, sem = first[half], P1 + (2 * i + half) * 6
            got(r1.at[i, half, 0, lo_rows], sem + 2)
            got(r1.at[i, half, 1, hi_rows], sem + 3)
            got(r1.at[i, half, 0, hi_rows], sem + 4)
            got(r1.at[i, half, 1, lo_rows], sem + 5)

            @pl.loop(0, 8)
            def _(b):
                rows = pl.ds(pl.multiple_of(b * 64, 64), 64)
                acc = part[i, half, a, rows].astype(F32)
                for k in range(2):
                    acc += r1[i, half, k, rows].astype(F32)
                part[i, half, a, rows] = acc.astype(BF)

            for k in (1, 2, 3):
                rows = pl.ds(pl.multiple_of(lax.rem(second[half] + k, 4) * 128, 128), 128)
                send(part.at[i, half, a, rows], r2.at[i, half, k - 1],
                     P2 + (2 * i + half) * 3 + k - 1, peer(1 - half, k))

    def reduce2(i):
        for half in (0, 1):
            a = first[half]
            for k in (1, 2, 3):
                got(r2.at[i, half, k - 1], P2 + (2 * i + half) * 3 + k - 1)

            def total(which):
                at = pl.ds(pl.multiple_of(second[half] * 128 + which * 64, 64), 64)
                rows = pl.ds(pl.multiple_of(which * 64, 64), 64)
                acc = part[i, half, a, at].astype(F32)
                for k in range(3):
                    acc += r2[i, half, k, rows].astype(F32)
                return acc

            x3[i, half] = total(1 - yl).astype(BF)
            cols = pl.ds(pl.multiple_of(half * INNER + (yl * 4 + i) * HD, HD), HD)
            send(x3.at[i, half], outb.at[:, cols], P3 + 2 * i + half, near)
            outb[:, cols] = total(yl).astype(BF)

    def finish(i):
        for half in (0, 1):
            cols = pl.ds(pl.multiple_of(half * INNER + ((1 - yl) * 4 + i) * HD, HD), HD)
            got(outb.at[:, cols], P3 + 2 * i + half)

    def enc_term(piece):
        @pl.loop(0, 2)
        def _(t):
            cols = pl.ds(pl.multiple_of(piece * 512 + t * 256, 256), 256)
            out = lax.dot_general(kv[...].reshape(512, 2 * INNER), w[cols, :], nt,
                                  preferred_element_type=F32).reshape(4, LEN, 256)
            for u in (0, 1):
                ek[u, :, cols] = jnp.where(c == 0, out[2 * u], out[2 * u + 1])
                es[u, :, cols] = jnp.where(c == 0, out[2 * u + 1], out[2 * u]).astype(BF)

        cols = pl.ds(piece * 512, 512)
        send(es.at[:, :, cols], er.at[:, :, cols], E1 + piece, core)

    def enc_pair(piece):
        cols = pl.ds(piece * 512, 512)
        got(er.at[:, :, cols], E1 + piece)
        ys[:, cols] = (ek[1 - yh, :, cols] + er[1 - yh, :, cols].astype(F32)).astype(BF)
        send(ys.at[:, cols], yr.at[:, cols], E2 + piece, partner)
        ek[yh, :, cols] = ek[yh, :, cols] + er[yh, :, cols].astype(F32)

    def enc_last(piece):
        cols = pl.ds(piece * 512, 512)
        got(yr.at[:, cols], E2 + piece)
        ek[yh, :, cols] = ek[yh, :, cols] + yr[:, cols].astype(F32)

    rest_kv(0)
    attend(0, 0)
    transpose(po)
    transpose(pp)
    transpose(ppo)
    rest_kv(1)
    got(encb.at[4 + p, low_rows], ENC + 2)
    send(encb.at[4 + p], encb.at[4 + p], ENC + 7, core)
    got(encb.at[4 + pp, top], ENC + 4)
    send(encb.at[4 + pp], encb.at[4 + pp], ENC + 8, core)
    send_factors(1)
    transpose(4 + p)
    transpose(4 + pp)
    got(encb.at[4 + po], ENC + 7)
    transpose(4 + po)
    got(encb.at[4 + ppo], ENC + 8)
    transpose(4 + ppo)
    weight(0, 0)
    attend(1, 1)
    direct(0)
    send_factors(2)
    rest_kv(2)
    beta(0)
    weight(1, 1)
    attend(2, 0)
    direct(1)
    send_factors(3)
    rest_kv(3)
    beta(1)
    weight(2, 0)
    attend(3, 1)
    direct(2)
    out_q = pltpu.make_async_copy(gqb, gq_hbm.at[0], lsem.at[3])
    out_q.start()
    reduce1(0)
    weight(3, 1)
    beta(2)
    direct(3)
    enc_term(0)
    reduce1(1)
    enc_term(1)
    enc_pair(0)
    reduce2(0)
    enc_term(2)
    beta(3)
    enc_pair(1)
    reduce1(2)
    enc_term(3)
    enc_pair(2)
    reduce2(1)
    reduce1(3)
    enc_pair(3)
    reduce2(2)
    reduce2(3)
    for piece in range(4):
        enc_last(piece)
    out_e = pltpu.make_async_copy(ek.at[yh], genc_hbm.at[0], lsem.at[4])
    out_e.start()
    for i in range(4):
        finish(i)
    out_w = pltpu.make_async_copy(outb, gkv_hbm.at[0], lsem.at[5])
    out_w.start()
    for cp in sends:
        cp.wait_send()
    out_q.wait()
    out_e.wait()
    out_w.wait()


def hand_over(gkv, genc, gq, gkv_out, genc_out, gq_out, low, wide, enc, query, isem, osem):
    loads = [pltpu.make_async_copy(src.at[0], dst, isem.at[n])
             for n, (src, dst) in enumerate(((gkv, low), (genc, enc), (gq, query)))]
    stores = [pltpu.make_async_copy(src, dst.at[0], osem.at[n])
              for n, (src, dst) in enumerate(((wide, gkv_out), (enc, genc_out), (query, gq_out)))]
    for cp in loads:
        cp.start()
    for n, (load, store) in enumerate(zip(loads, stores)):
        load.wait()
        if n == 0:
            @pl.loop(0, 8)
            def _(b):
                cols = pl.ds(pl.multiple_of(b * 512, 512), 512)
                wide[:, cols] = low[:, cols].astype(F32)
        store.start()
    for cp in stores:
        cp.wait()


def per_device(enc_out, kv_weight, queries, out_grad):
    anywhere = pl.BlockSpec(memory_space=pl.ANY)
    vm = pltpu.VMEM
    gkv, genc, gq = pl.pallas_call(
        body,
        out_shape=(
            jax.ShapeDtypeStruct((1, 64, 2 * INNER), BF),
            jax.ShapeDtypeStruct((1, LEN, D), F32),
            jax.ShapeDtypeStruct((1, 4, Q, INNER), BF),
        ),
        in_specs=[anywhere] * 4,
        out_specs=(anywhere,) * 3,
        scratch_shapes=[
            vm((D, 2 * INNER), BF),
            vm((8, LEN, D), BF),
            vm((D, 8 * LEN), BF),
            vm((4, LEN, 2 * INNER), BF),
            vm((4, Q, INNER), BF),
            vm((4, Q, INNER), BF),
            vm((4, 2, 4, Q, HD), BF),
            vm((4, Q, INNER), BF),
            vm((4, 2, 4, Q, LEN), BF),
            vm((4, 2, 4, Q, LEN), BF),
            vm((2, 8 * LEN, 2 * HD), BF),
            vm((4, 2, 4, 512, HD), BF),
            vm((4, 2, 2, 256, HD), BF),
            vm((4, 2, 2, 512, HD), BF),
            vm((4, 2, 3, 128, HD), BF),
            vm((4, 2, 64, HD), BF),
            vm((64, 2 * INNER), BF),
            vm((2, LEN, D), F32),
            vm((2, LEN, D), BF),
            vm((2, LEN, D), BF),
            vm((LEN, D), BF),
            vm((LEN, D), BF),
            pltpu.SemaphoreType.DMA((6,)),
            pltpu.SemaphoreType.DMA((16,)),
            pltpu.SemaphoreType.DMA((NSEM,)),
            pltpu.SemaphoreType.DMA((NSEM,)),
        ],
        compiler_params=pltpu.CompilerParams(
            collective_id=0, has_side_effects=True, vmem_limit_bytes=62 * 1024 * 1024),
        name="kv_backward",
    )(enc_out, kv_weight, queries, out_grad)
    return pl.pallas_call(
        hand_over,
        out_shape=(
            jax.ShapeDtypeStruct((1, 64, 2 * INNER), F32),
            jax.ShapeDtypeStruct((1, LEN, D), F32),
            jax.ShapeDtypeStruct((1, 4, Q, INNER), BF),
        ),
        in_specs=[anywhere] * 3,
        out_specs=(anywhere,) * 3,
        scratch_shapes=[
            vm((64, 2 * INNER), BF),
            vm((64, 2 * INNER), F32),
            vm((LEN, D), F32),
            vm((4, Q, INNER), BF),
            pltpu.SemaphoreType.DMA((3,)),
            pltpu.SemaphoreType.DMA((3,)),
        ],
        compiler_params=pltpu.CompilerParams(vmem_limit_bytes=16 * 1024 * 1024),
        name="hand_over",
    )(gkv, genc, gq)


def solution(mesh):
    placed = (
        P("pipe", "dp", None),
        P("pipe", None, None),
        P("pipe", None, "dp", None),
        P("pipe", None, "dp", None),
    )
    return jax.shard_map(
        per_device,
        mesh=mesh,
        in_specs=placed,
        out_specs=(P("pipe", "dp", None), P("pipe", "dp", None), P("pipe", None, "dp", None)),
        check_vma=False,
    )
```

```python
import jax
import jax.numpy as jnp
from jax import lax
from jax.experimental import pallas as pl
from jax.experimental.pallas import tpu as pltpu
from jax.sharding import PartitionSpec as P

HD = 256
INNER = 2048
D = 2048
LEN = 128
Q = 32
BF = jnp.bfloat16
F32 = jnp.float32
MESH = pl.DeviceIdType.MESH

ENC, QG, SC, P1, P2, P3, E1, E2, NSEM = 0, 10, 18, 22, 70, 94, 102, 106, 110


def body(enc_hbm, w_hbm, q_hbm, g_hbm, gkv_hbm, genc_hbm, gq_hbm,
         w, encb, enct, kv, qb, gb, qgn, gqb, sco, sci, rhs, part, f1, r1, r2, x3, outb,
         ek, es, er, ys, yr, lsem, wsem, ssem, rsem):
    p = lax.axis_index("pipe")
    d = lax.axis_index("dp")
    yh, c = p // 2, p % 2
    x, yl, z = d // 8, (d // 4) % 2, d % 4
    po = 2 * yh + 1 - c
    pp = 2 * (1 - yh) + c
    ppo = 2 * (1 - yh) + 1 - c
    dn = x * 8 + (1 - yl) * 4 + z
    core, partner, near, far = (po, d), (pp, d), (p, dn), (pp, dn)

    def peer(half_axis, k):
        if half_axis == 0:
            return (p, lax.rem(x + k, 4) * 8 + yl * 4 + z)
        return (p, x * 8 + yl * 4 + lax.rem(z + k, 4))

    def rc(src, dst, idx, dev):
        return pltpu.make_async_remote_copy(
            src_ref=src, dst_ref=dst, send_sem=ssem.at[idx], recv_sem=rsem.at[idx],
            device_id=dev, device_id_type=MESH)

    def got(dst, idx):
        rc(dst, dst, idx, core).wait_recv()

    def w_copy(j):
        cols = pl.ds(pl.multiple_of(j * 256, 256), 256)
        return pltpu.make_async_copy(w_hbm.at[0, :, cols], w.at[:, cols], wsem.at[j])

    own_enc = pltpu.make_async_copy(enc_hbm.at[0], encb.at[p], lsem.at[0])
    own_q = pltpu.make_async_copy(q_hbm.at[0], qb, lsem.at[1])
    own_g = pltpu.make_async_copy(g_hbm.at[0], gb, lsem.at[2])
    own_enc.start()

    @pl.loop(0, 16)
    def _(j):
        w_copy(j).start()

    own_q.start()
    own_g.start()

    barrier = pltpu.get_barrier_semaphore()
    others = [core, partner, near, far] + [peer(h, k) for h in (0, 1) for k in (1, 2, 3)]
    for dev in others:
        pl.semaphore_signal(barrier, inc=1, device_id=dev, device_id_type=MESH)
    pl.semaphore_wait(barrier, len(others))

    sends = []

    def send(src, dst, idx, dev):
        cp = rc(src, dst, idx, dev)
        cp.start()
        sends.append(cp)

    top, low_rows = pl.ds(0, 64), pl.ds(64, 64)
    send(enc_hbm.at[0], encb.at[p], ENC + 0, core)
    send(enc_hbm.at[0, top], encb.at[4 + p, top], ENC + 1, near)
    send(enc_hbm.at[0, low_rows], encb.at[4 + p, low_rows], ENC + 3, far)

    def project(first, j):
        cols = pl.ds(pl.multiple_of(j * 256, 256), 256)
        rows = encb[pl.ds(first, 2)].reshape(256, D)
        out = jnp.dot(rows, w[:, cols], preferred_element_type=F32)
        kv[pl.ds(first, 2), :, cols] = out.astype(BF).reshape(2, LEN, 256)

    def transpose(slot):
        cols = pl.ds(pl.multiple_of(slot * LEN, LEN), LEN)

        @pl.loop(0, 8)
        def _(b):
            rows = pl.ds(pl.multiple_of(b * 256, 256), 256)
            enct[rows, cols] = encb[slot, :, rows].T

    own_enc.wait()
    got(encb.at[po], ENC + 0)

    def local_kv(lo, hi):
        @pl.loop(lo, hi)
        def _(j):
            w_copy(j).wait()
            project(2 * yh, j)

    def send_factors(i):
        cols = pl.ds(pl.multiple_of((1 - yl) * 1024 + i * 256, 256), 256)
        send(qb.at[:, :, cols], qgn.at[i, 0], QG + 2 * i, near)
        send(gb.at[:, :, cols], qgn.at[i, 1], QG + 2 * i + 1, near)

    local_kv(0, 4)
    got(encb.at[4 + p, top], ENC + 1)
    send(encb.at[4 + p, top], encb.at[p, top], ENC + 5, far)
    got(encb.at[4 + pp, low_rows], ENC + 3)
    send(encb.at[4 + pp, low_rows], encb.at[pp, low_rows], ENC + 6, near)
    own_q.wait()
    own_g.wait()
    local_kv(4, 13)
    got(encb.at[pp, top], ENC + 5)
    got(encb.at[pp, low_rows], ENC + 6)
    send(encb.at[pp], encb.at[pp], ENC + 9, core)
    send(enc_hbm.at[0, low_rows], encb.at[4 + p, low_rows], ENC + 2, near)
    send(enc_hbm.at[0, top], encb.at[4 + p, top], ENC + 4, far)
    send_factors(0)
    local_kv(13, 16)
    transpose(p)
    got(encb.at[ppo], ENC + 9)

    tl = (((0,), (0,)), ((), ()))
    nt = (((1,), (1,)), ((), ()))

    def rest_kv(i):
        @pl.loop(0, 4)
        def _(t):
            project(2 * (1 - yh), i + 4 * t)

    def attend(i, slot):
        units = []
        for own in (0, 1):
            head = (yl if own else 1 - yl) * 4 + i
            kc = pl.ds(pl.multiple_of(head * HD, HD), HD)
            vc = pl.ds(pl.multiple_of(INNER + head * HD, HD), HD)
            for m in range(4):
                units.append((own, kc, vc, m))
        raws, pgs = [], []
        for own, kc, vc, m in units:
            raws.append(lax.dot_general(qb[m, :, kc], kv[m, :, kc], nt, preferred_element_type=F32))
            pgs.append(lax.dot_general(gb[m, :, kc], kv[m, :, vc], nt, preferred_element_type=F32))
        raw = jnp.concatenate(raws, axis=0)
        pg = jnp.concatenate(pgs, axis=0)
        e = jnp.exp(raw - jnp.max(raw, axis=-1, keepdims=True))
        prob = e / jnp.sum(e, axis=-1, keepdims=True)
        total = jnp.sum(prob * pg, axis=-1, keepdims=True)
        score = (prob * (pg - total)).astype(BF)
        low = prob.astype(BF)
        for n, (own, kc, vc, m) in enumerate(units):
            s_n, p_n = score[n * Q:(n + 1) * Q], low[n * Q:(n + 1) * Q]
            gqb[m, :, kc] = jnp.dot(s_n, kv[m, :, kc], preferred_element_type=F32).astype(BF)
            kg = lax.dot_general(s_n, qb[m, :, kc], tl, preferred_element_type=F32).astype(BF)
            vg = lax.dot_general(p_n, gb[m, :, kc], tl, preferred_element_type=F32).astype(BF)
            kv[m, :, kc] = kg
            kv[m, :, vc] = vg
            if own:
                rhs[slot, m * LEN:(m + 1) * LEN, 0:HD] = kg
                rhs[slot, m * LEN:(m + 1) * LEN, HD:2 * HD] = vg
            else:
                sco[i, 0, m] = s_n
                sco[i, 1, m] = p_n
        send(sco.at[i], sci.at[i], SC + i, near)

    def weight(i, slot):
        got(sci.at[i], SC + i)
        got(qgn.at[i, 0], QG + 2 * i)
        got(qgn.at[i, 1], QG + 2 * i + 1)
        for m in range(4):
            kg = lax.dot_general(sci[i, 0, m], qgn[i, 0, m], tl, preferred_element_type=F32)
            vg = lax.dot_general(sci[i, 1, m], qgn[i, 1, m], tl, preferred_element_type=F32)
            rhs[slot, 512 + m * LEN:512 + (m + 1) * LEN, 0:HD] = kg.astype(BF)
            rhs[slot, 512 + m * LEN:512 + (m + 1) * LEN, HD:2 * HD] = vg.astype(BF)

        for half in (0, 1):
            @pl.loop(0, 4)
            def _(xp):
                rows = pl.ds(pl.multiple_of(xp * 512, 512), 512)
                out = jnp.dot(enct[rows, :], rhs[slot, :, half * HD:(half + 1) * HD],
                              preferred_element_type=F32).astype(BF)
                for yy in range(2):
                    for zz in range(4):
                        piece = out[yy * 256 + zz * 64:yy * 256 + zz * 64 + 64]
                        if half == 0:
                            part[i, 0, xp, zz * 128 + yy * 64:zz * 128 + yy * 64 + 64] = piece
                        else:
                            at = pl.multiple_of(xp * 128 + yy * 64, 64)
                            part[i, 1, zz, pl.ds(at, 64)] = piece

            alpha(i, half)

    first = (x, z)
    second = (z, x)

    hi_rows, lo_rows = pl.ds(0, 256), pl.ds(256, 256)

    def alpha(i, half):
        a, sem = first[half], P1 + (2 * i + half) * 6
        across = lax.rem(a + 2, 4)
        send(part.at[i, half, across, hi_rows], f1.at[i, half, 0], sem, peer(half, 1))
        send(part.at[i, half, across, lo_rows], f1.at[i, half, 1], sem + 1, peer(half, 3))

    def direct(i):
        for half in (0, 1):
            a, sem = first[half], P1 + (2 * i + half) * 6
            up, down = lax.rem(a + 1, 4), lax.rem(a + 3, 4)
            send(part.at[i, half, up, lo_rows], r1.at[i, half, 0, lo_rows], sem + 2, peer(half, 1))
            send(part.at[i, half, down, hi_rows], r1.at[i, half, 1, hi_rows], sem + 3, peer(half, 3))

    def beta(i):
        for half in (0, 1):
            a, sem = first[half], P1 + (2 * i + half) * 6
            for way, rows, k in ((0, hi_rows, 1), (1, lo_rows, 3)):
                got(f1.at[i, half, way], sem + way)
                block = lax.rem(a + k, 4)

                @pl.loop(0, 4)
                def _(b):
                    src = pl.ds(pl.multiple_of(b * 64, 64), 64)
                    dst = pl.ds(pl.multiple_of(way * 256 + b * 64, 64), 64)
                    acc = part[i, half, block, dst].astype(F32) + f1[i, half, way, src].astype(F32)
                    part[i, half, block, dst] = acc.astype(BF)

                send(part.at[i, half, block, rows], r1.at[i, half, way, rows], sem + 4 + way,
                     peer(half, k))

    def reduce1(i):
        for half in (0, 1):
            a, sem = first[half], P1 + (2 * i + half) * 6
            got(r1.at[i, half, 0, lo_rows], sem + 2)
            got(r1.at[i, half, 1, hi_rows], sem + 3)
            got(r1.at[i, half, 0, hi_rows], sem + 4)
            got(r1.at[i, half, 1, lo_rows], sem + 5)

            @pl.loop(0, 8)
            def _(b):
                rows = pl.ds(pl.multiple_of(b * 64, 64), 64)
                acc = part[i, half, a, rows].astype(F32)
                for k in range(2):
                    acc += r1[i, half, k, rows].astype(F32)
                part[i, half, a, rows] = acc.astype(BF)

            for k in (1, 2, 3):
                rows = pl.ds(pl.multiple_of(lax.rem(second[half] + k, 4) * 128, 128), 128)
                send(part.at[i, half, a, rows], r2.at[i, half, k - 1],
                     P2 + (2 * i + half) * 3 + k - 1, peer(1 - half, k))

    def reduce2(i):
        for half in (0, 1):
            a = first[half]
            for k in (1, 2, 3):
                got(r2.at[i, half, k - 1], P2 + (2 * i + half) * 3 + k - 1)

            def total(which):
                at = pl.ds(pl.multiple_of(second[half] * 128 + which * 64, 64), 64)
                rows = pl.ds(pl.multiple_of(which * 64, 64), 64)
                acc = part[i, half, a, at].astype(F32)
                for k in range(3):
                    acc += r2[i, half, k, rows].astype(F32)
                return acc

            x3[i, half] = total(1 - yl).astype(BF)
            cols = pl.ds(pl.multiple_of(half * INNER + (yl * 4 + i) * HD, HD), HD)
            send(x3.at[i, half], outb.at[:, cols], P3 + 2 * i + half, near)
            outb[:, cols] = total(yl).astype(BF)

    def finish(i):
        for half in (0, 1):
            cols = pl.ds(pl.multiple_of(half * INNER + ((1 - yl) * 4 + i) * HD, HD), HD)
            got(outb.at[:, cols], P3 + 2 * i + half)

    def enc_term(piece):
        @pl.loop(0, 2)
        def _(t):
            cols = pl.ds(pl.multiple_of(piece * 512 + t * 256, 256), 256)
            out = lax.dot_general(kv[...].reshape(512, 2 * INNER), w[cols, :], nt,
                                  preferred_element_type=F32).reshape(4, LEN, 256)
            for u in (0, 1):
                ek[u, :, cols] = jnp.where(c == 0, out[2 * u], out[2 * u + 1])
                es[u, :, cols] = jnp.where(c == 0, out[2 * u + 1], out[2 * u]).astype(BF)

        cols = pl.ds(piece * 512, 512)
        send(es.at[:, :, cols], er.at[:, :, cols], E1 + piece, core)

    def enc_pair(piece):
        cols = pl.ds(piece * 512, 512)
        got(er.at[:, :, cols], E1 + piece)
        ys[:, cols] = (ek[1 - yh, :, cols] + er[1 - yh, :, cols].astype(F32)).astype(BF)
        send(ys.at[:, cols], yr.at[:, cols], E2 + piece, partner)
        ek[yh, :, cols] = ek[yh, :, cols] + er[yh, :, cols].astype(F32)

    def enc_last(piece):
        cols = pl.ds(piece * 512, 512)
        got(yr.at[:, cols], E2 + piece)
        ek[yh, :, cols] = ek[yh, :, cols] + yr[:, cols].astype(F32)

    rest_kv(0)
    attend(0, 0)
    transpose(po)
    transpose(pp)
    transpose(ppo)
    rest_kv(1)
    got(encb.at[4 + p, low_rows], ENC + 2)
    send(encb.at[4 + p], encb.at[4 + p], ENC + 7, core)
    got(encb.at[4 + pp, top], ENC + 4)
    send(encb.at[4 + pp], encb.at[4 + pp], ENC + 8, core)
    send_factors(1)
    transpose(4 + p)
    transpose(4 + pp)
    got(encb.at[4 + po], ENC + 7)
    transpose(4 + po)
    got(encb.at[4 + ppo], ENC + 8)
    transpose(4 + ppo)
    weight(0, 0)
    attend(1, 1)
    direct(0)
    send_factors(2)
    rest_kv(2)
    beta(0)
    weight(1, 1)
    attend(2, 0)
    direct(1)
    send_factors(3)
    rest_kv(3)
    beta(1)
    weight(2, 0)
    attend(3, 1)
    direct(2)
    out_q = pltpu.make_async_copy(gqb, gq_hbm.at[0], lsem.at[3])
    out_q.start()
    reduce1(0)
    weight(3, 1)
    beta(2)
    direct(3)
    enc_term(0)
    reduce1(1)
    enc_term(1)
    enc_pair(0)
    reduce2(0)
    enc_term(2)
    beta(3)
    enc_pair(1)
    reduce1(2)
    enc_term(3)
    enc_pair(2)
    reduce2(1)
    enc_pair(3)
    reduce1(3)
    reduce2(2)
    reduce2(3)
    for piece in range(4):
        enc_last(piece)
    out_e = pltpu.make_async_copy(ek.at[yh], genc_hbm.at[0], lsem.at[4])
    out_e.start()
    for i in range(4):
        finish(i)
    out_w = pltpu.make_async_copy(outb, gkv_hbm.at[0], lsem.at[5])
    out_w.start()
    for cp in sends:
        cp.wait_send()
    out_q.wait()
    out_e.wait()
    out_w.wait()


def hand_over(gkv, genc, gq, gkv_out, genc_out, gq_out, low, wide, enc, query, isem, osem):
    loads = [pltpu.make_async_copy(src.at[0], dst, isem.at[n])
             for n, (src, dst) in enumerate(((gkv, low), (genc, enc), (gq, query)))]
    stores = [pltpu.make_async_copy(src, dst.at[0], osem.at[n])
              for n, (src, dst) in enumerate(((wide, gkv_out), (enc, genc_out), (query, gq_out)))]
    for cp in loads:
        cp.start()
    for n, (load, store) in enumerate(zip(loads, stores)):
        load.wait()
        if n == 0:
            @pl.loop(0, 8)
            def _(b):
                cols = pl.ds(pl.multiple_of(b * 512, 512), 512)
                wide[:, cols] = low[:, cols].astype(F32)
        store.start()
    for cp in stores:
        cp.wait()


def per_device(enc_out, kv_weight, queries, out_grad):
    anywhere = pl.BlockSpec(memory_space=pl.ANY)
    vm = pltpu.VMEM
    gkv, genc, gq = pl.pallas_call(
        body,
        out_shape=(
            jax.ShapeDtypeStruct((1, 64, 2 * INNER), BF),
            jax.ShapeDtypeStruct((1, LEN, D), F32),
            jax.ShapeDtypeStruct((1, 4, Q, INNER), BF),
        ),
        in_specs=[anywhere] * 4,
        out_specs=(anywhere,) * 3,
        scratch_shapes=[
            vm((D, 2 * INNER), BF),
            vm((8, LEN, D), BF),
            vm((D, 8 * LEN), BF),
            vm((4, LEN, 2 * INNER), BF),
            vm((4, Q, INNER), BF),
            vm((4, Q, INNER), BF),
            vm((4, 2, 4, Q, HD), BF),
            vm((4, Q, INNER), BF),
            vm((4, 2, 4, Q, LEN), BF),
            vm((4, 2, 4, Q, LEN), BF),
            vm((2, 8 * LEN, 2 * HD), BF),
            vm((4, 2, 4, 512, HD), BF),
            vm((4, 2, 2, 256, HD), BF),
            vm((4, 2, 2, 512, HD), BF),
            vm((4, 2, 3, 128, HD), BF),
            vm((4, 2, 64, HD), BF),
            vm((64, 2 * INNER), BF),
            vm((2, LEN, D), F32),
            vm((2, LEN, D), BF),
            vm((2, LEN, D), BF),
            vm((LEN, D), BF),
            vm((LEN, D), BF),
            pltpu.SemaphoreType.DMA((6,)),
            pltpu.SemaphoreType.DMA((16,)),
            pltpu.SemaphoreType.DMA((NSEM,)),
            pltpu.SemaphoreType.DMA((NSEM,)),
        ],
        compiler_params=pltpu.CompilerParams(
            collective_id=0, has_side_effects=True, vmem_limit_bytes=62 * 1024 * 1024),
        name="kv_backward",
    )(enc_out, kv_weight, queries, out_grad)
    return pl.pallas_call(
        hand_over,
        out_shape=(
            jax.ShapeDtypeStruct((1, 64, 2 * INNER), F32),
            jax.ShapeDtypeStruct((1, LEN, D), F32),
            jax.ShapeDtypeStruct((1, 4, Q, INNER), BF),
        ),
        in_specs=[anywhere] * 3,
        out_specs=(anywhere,) * 3,
        scratch_shapes=[
            vm((64, 2 * INNER), BF),
            vm((64, 2 * INNER), F32),
            vm((LEN, D), F32),
            vm((4, Q, INNER), BF),
            pltpu.SemaphoreType.DMA((3,)),
            pltpu.SemaphoreType.DMA((3,)),
        ],
        compiler_params=pltpu.CompilerParams(vmem_limit_bytes=16 * 1024 * 1024),
        name="hand_over",
    )(gkv, genc, gq)


def solution(mesh):
    placed = (
        P("pipe", "dp", None),
        P("pipe", None, None),
        P("pipe", None, "dp", None),
        P("pipe", None, "dp", None),
    )
    return jax.shard_map(
        per_device,
        mesh=mesh,
        in_specs=placed,
        out_specs=(P("pipe", "dp", None), P("pipe", "dp", None), P("pipe", None, "dp", None)),
        check_vma=False,
    )
```
